32 devices in a mesh: surf: 8 (over y, x, core), wall: 4 (over z).
Axes of the slice: x: 2, y: 2, z: 4, core: 2. Of those that a mesh axis runs over, the one named last changes fastest.
Arguments:
- flow_state: float32 [5, 128, 64, 512], P(None, 'wall', 'surf'), may hold values from -1 to 6, as said below
- spacing: float32 [128, 64, 512], P('wall', 'surf'), may hold values from 0.6 to 1.8
- bc_kind: int32 [64, 512], P('surf'), may hold values from 0 to 2
- cell_of: int32 [32768], P(('surf', 'wall')), may hold values from 0 to 32767, as said below
- zone_id: int32 [32768], P(('surf', 'wall')), may hold values from 0 to 7
- abl_temp: float32 [64, 32768], P(None, ('surf', 'wall')), may hold values from 0.5 to 2
- conduct: float32 [8], replicated, may hold values from 0.3 to 3
- diffuse: float32 [8], replicated, may hold values from 0.1 to 0.45
- rate: float32 [8], replicated, may hold values from 0.3 to 3
Outputs:
- state_next: float32 [5, 128, 64, 512], P(None, 'wall', 'surf')
- node_shift: float32 [128, 64, 512], P('wall', 'surf')
- ablator_next: float32 [64, 32768], P(None, ('surf', 'wall'))
The draws below stay inside these ranges and needn't reach their ends.
Inputs may be any that keep to these rules, and one draw needn't show every extreme that they name: `cell_of`: each surface cell is named by exactly one column; the columns of one device name exactly 128 cells of every surface tile (tile = cell // 4096). `flow_state`: the density U0 is at least 0.45 and the pressure derived from U is at least 0.37 in every cell.
All inputs are finite; a program needn't handle non-finite values.
Results may differ from the reference program's by a relative error of at most 0.0003.
Values sent between devices are 32-bit elements; how exact they have to be, the bound alone decides.
A program may use at most 128 MiB of HBM per device.

```python
import math
import jax
import jax.numpy as jnp
from jax import lax

CI = 8
NJ = 512
DEPTH = 64
NZONE = 8
NI = 64
NK = 128
NCOL = 32768
N_SURF = 8
N_WALL = 4


def draw_flow_state(key, part):
    keys = jax.random.split(key, 5)
    shape = (NK, NI, NJ)
    density = jax.random.uniform(keys[0], shape, jnp.float32, 0.7, 1.3)
    velo_x = 0.3 * jax.random.truncated_normal(keys[1], -2.0, 2.0, shape, jnp.float32)
    velo_y = 0.3 * jax.random.truncated_normal(keys[2], -2.0, 2.0, shape, jnp.float32)
    velo_z = 0.3 * jax.random.truncated_normal(keys[3], -2.0, 2.0, shape, jnp.float32)
    pressure = jax.random.uniform(keys[4], shape, jnp.float32, 0.6, 1.4)
    energy = pressure / 0.4 + 0.5 * density * (velo_x * velo_x + velo_y * velo_y + velo_z * velo_z)
    return jnp.stack([density, density * velo_x, density * velo_y, density * velo_z, energy])


def tile_pieces(tile_key, tile_index):
    tile_cells = CI * NJ
    device_count = N_SURF * N_WALL
    shuffled = jax.random.permutation(tile_key, tile_cells).astype(jnp.int32) + tile_index * tile_cells
    return shuffled.reshape(device_count, tile_cells // device_count)


def mix_row(row_key, row_values):
    return jax.random.permutation(row_key, row_values)


def draw_cell_of(key, part):
    device_count = N_SURF * N_WALL
    tile_keys = jax.random.split(jax.random.fold_in(key, 11), N_SURF)
    pieces = jax.vmap(tile_pieces)(tile_keys, jnp.arange(N_SURF, dtype=jnp.int32))
    per_device = jnp.transpose(pieces, (1, 0, 2)).reshape(device_count, -1)
    device_keys = jax.random.split(jax.random.fold_in(key, 23), device_count)
    mixed = jax.vmap(mix_row)(device_keys, per_device)
    return mixed.reshape(-1).astype(jnp.int32)


def set_ends(entries, key, low, high):
    shape = entries.shape
    index_at = [jax.random.randint(jax.random.fold_in(key, axis), (), 0, shape[axis]) for axis in range(len(shape))]
    entries = entries.at[tuple(index_at)].set(low)
    longest = shape.index(max(shape))
    index_at[longest] = (index_at[longest] + 1) % shape[longest]
    return entries.at[tuple(index_at)].set(high)


def level_of(own_key, shape, cuts, least, largest):
    loudness = 1.0
    for axis_at, shards_of in cuts:
        heights = jax.random.uniform(jax.random.fold_in(jax.random.fold_in(own_key, 6), axis_at), (shards_of,), jnp.float32, least / len(cuts), largest / len(cuts))
        loudness = loudness * jnp.repeat(jnp.exp(heights), shape[axis_at] // shards_of).reshape((-1,) + (1,) * (len(shape) - 1 - axis_at))
    return loudness


def setup_inputs(seed: int = 0) -> dict:
    key_of = jax.random.split(jax.random.key(seed), 10)
    return {
        "flow_state": draw_flow_state(jax.random.fold_in(key_of[9], 71), 0),
        "spacing": jnp.clip(0.6 + 1.1999999 * jax.random.uniform(key_of[1], (NK, NI, NJ), jnp.float32) ** level_of(key_of[1], (NK, NI, NJ), ((0, 4), (1, 8)), -0.2, 0.2), 0.6, 1.8),
        "bc_kind": set_ends(jax.random.randint(key_of[2], (NI, NJ), 0, 3), jax.random.fold_in(key_of[2], 1), 0, 2).astype(jnp.int32),
        "cell_of": draw_cell_of(jax.random.fold_in(key_of[9], 71), 0),
        "zone_id": set_ends(jax.random.randint(key_of[4], (NCOL,), 0, NZONE), jax.random.fold_in(key_of[4], 1), 0, NZONE - 1).astype(jnp.int32),
        "abl_temp": jnp.clip(0.5 + 1.5 * jax.random.uniform(key_of[5], (DEPTH, NCOL), jnp.float32) ** level_of(key_of[5], (DEPTH, NCOL), ((1, 32),), -0.2, 0.2), 0.5, 2.0),
        "conduct": jnp.clip(jnp.exp(jax.random.uniform(key_of[6], (NZONE,), jnp.float32, math.log(0.3), math.log(3.0))), 0.3, 3.0),
        "diffuse": jnp.clip(jax.random.uniform(key_of[7], (NZONE,), jnp.float32, 0.1, 0.45), 0.1, 0.45),
        "rate": jnp.clip(jnp.exp(jax.random.uniform(key_of[8], (NZONE,), jnp.float32, math.log(0.3), math.log(3.0))), 0.3, 3.0),
    }


heat_ratio = 1.4
time_step = 0.15
viscosity = 0.05
conduction = 0.07
sponge_rate = 0.5
activation = 2.0
blow_ratio = 1.0
radiation = 0.8
film_conduct = 1.0
recovery = 0.2
far_values = (1.0, 0.5, 0.0, 0.0, 2.625)


def primitives(values):
    density = values[0]
    velo_x = values[1] / density
    velo_y = values[2] / density
    velo_z = values[3] / density
    kinetic = 0.5 * density * (velo_x * velo_x + velo_y * velo_y + velo_z * velo_z)
    pressure = (heat_ratio - 1.0) * (values[4] - kinetic)
    return density, velo_x, velo_y, velo_z, pressure


def conserved(density, velo_x, velo_y, velo_z, pressure):
    energy = pressure / (heat_ratio - 1.0) + 0.5 * density * (velo_x * velo_x + velo_y * velo_y + velo_z * velo_z)
    return jnp.stack([density, density * velo_x, density * velo_y, density * velo_z, energy])


def wall_ghost(cell_row, surf_temp, surf_blow, kind_rows):
    density, velo_x, velo_y, velo_z, pressure = primitives(cell_row)
    wall_density = pressure / surf_temp
    noslip = conserved(wall_density, -velo_x, -velo_y, -velo_z, pressure)
    slip_state = conserved(density, velo_x, velo_y, -velo_z, pressure)
    blow_state = conserved(wall_density, -velo_x, -velo_y, 2.0 * surf_blow - velo_z, pressure)
    return jnp.where(kind_rows == 0, noslip, jnp.where(kind_rows == 1, slip_state, blow_state))


def shifted_slice(padded, along_axis, offset, length):
    return lax.slice_in_dim(padded, 2 + offset, 2 + offset + length, axis=along_axis)


def first_diff(padded, along_axis, length):
    near_diff = shifted_slice(padded, along_axis, 1, length) - shifted_slice(padded, along_axis, -1, length)
    outer_diff = shifted_slice(padded, along_axis, 2, length) - shifted_slice(padded, along_axis, -2, length)
    return (8.0 * near_diff - outer_diff) / 12.0


def second_diff(padded, along_axis, length):
    near_sum = shifted_slice(padded, along_axis, 1, length) + shifted_slice(padded, along_axis, -1, length)
    outer_sum = shifted_slice(padded, along_axis, 2, length) + shifted_slice(padded, along_axis, -2, length)
    return (16.0 * near_sum - outer_sum - 30.0 * shifted_slice(padded, along_axis, 0, length)) / 12.0


def wrap_last(values):
    return jnp.concatenate([values[..., -2:], values, values[..., :2]], axis=-1)


def fluxes(values, normal):
    density, velo_x, velo_y, velo_z, pressure = primitives(values)
    speeds = (velo_x, velo_y, velo_z)
    normal_speed = speeds[normal]
    momentum_flux = [values[1] * normal_speed, values[2] * normal_speed, values[3] * normal_speed]
    momentum_flux[normal] = momentum_flux[normal] + pressure
    face_flux = jnp.stack([values[normal + 1], momentum_flux[0], momentum_flux[1], momentum_flux[2], (values[4] + pressure) * normal_speed])
    lap_fields = jnp.stack([velo_x, velo_y, velo_z, pressure / density])
    return face_flux, lap_fields


def advance(padded_state, padded_heights, normalized):
    depth_k = padded_heights.shape[0] - 4
    rows_i = padded_state.shape[2] - 4
    cols_j = padded_state.shape[3]
    center_state = padded_state[:, 2:-2, 2:-2, :]
    side_state = padded_state[:, 2:-2, :, :]
    stack_state = padded_state[:, :, 2:-2, :]
    flux_i, lap_i = fluxes(side_state, 0)
    flux_j, lap_j = fluxes(wrap_last(center_state), 1)
    flux_k, lap_k = fluxes(stack_state, 2)
    metric = first_diff(padded_heights, 0, depth_k)
    convect = first_diff(flux_i, 2, rows_i) + first_diff(flux_j, 3, cols_j) + first_diff(flux_k, 1, depth_k) / metric
    laplace = second_diff(lap_i, 2, rows_i) + second_diff(lap_j, 3, cols_j) + second_diff(lap_k, 1, depth_k) / (metric * metric)
    viscous = jnp.stack([jnp.zeros_like(laplace[0]), viscosity * laplace[0], viscosity * laplace[1], viscosity * laplace[2], conduction * laplace[3]])
    far_field = jnp.array(far_values, jnp.float32)[:, None, None, None]
    sponge = sponge_rate * normalized * normalized * (center_state - far_field)
    return center_state + time_step * (viscous - convect - sponge)


def ablate(abl_temp, col_film, col_recovery, col_conduct, col_diffuse, col_rate):
    inner_temp = abl_temp[1]
    surface = abl_temp[0]
    for newton_pass in range(2):
        surface_cube = surface * surface * surface
        surface = (col_film * col_recovery + col_conduct * inner_temp + 3.0 * radiation * surface_cube * surface) / (col_film + col_conduct + 4.0 * radiation * surface_cube)
    recession = col_rate * jnp.exp(-activation / surface)
    blowing = blow_ratio * recession
    profile = jnp.concatenate([surface[None], abl_temp[1:]], axis=0)
    for heat_pass in range(2):
        middle = profile[1:-1] + col_diffuse * (profile[2:] - 2.0 * profile[1:-1] + profile[:-2])
        bottom = profile[-1] + 2.0 * col_diffuse * (profile[-2] - profile[-1])
        profile = jnp.concatenate([profile[:1], middle, bottom[None]], axis=0)
    return surface, blowing, recession, profile


def extend_heights(shifted):
    wall_low = jnp.stack([3.0 * shifted[0] - 2.0 * shifted[1], 2.0 * shifted[0] - shifted[1]])
    wall_high = jnp.stack([2.0 * shifted[-1] - shifted[-2], 3.0 * shifted[-1] - 2.0 * shifted[-2]])
    return jnp.concatenate([wall_low, shifted, wall_high], axis=0)


def reference(flow_state, spacing, bc_kind, cell_of, zone_id, abl_temp, conduct, diffuse, rate):
    density, velo_x, velo_y, velo_z, pressure = primitives(flow_state[:, 0])
    recovery_temp = pressure / density + recovery * (velo_x * velo_x + velo_y * velo_y + velo_z * velo_z)
    film = film_conduct / (0.5 * spacing[0])
    col_film = film.reshape(-1)[cell_of]
    col_recovery = recovery_temp.reshape(-1)[cell_of]
    surface, blowing, recession, ablator_next = ablate(abl_temp, col_film, col_recovery, conduct[zone_id], diffuse[zone_id], rate[zone_id])
    cell_count = NI * NJ
    surf_temp = jnp.zeros((cell_count,), jnp.float32).at[cell_of].set(surface).reshape(NI, NJ)
    surf_blow = jnp.zeros((cell_count,), jnp.float32).at[cell_of].set(blowing).reshape(NI, NJ)
    surf_recess = jnp.zeros((cell_count,), jnp.float32).at[cell_of].set(recession).reshape(NI, NJ)
    center = jnp.cumsum(spacing, axis=0) - 0.5 * spacing
    column_total = jnp.sum(spacing, axis=0)
    node_shift = surf_recess * (center / column_total - 1.0)
    shifted = center + node_shift
    normalized = center / column_total

    def one_tile(tile_index):
        first_row = tile_index * CI
        wrapped = (first_row - 2 + jnp.arange(CI + 4, dtype=jnp.int32)) % NI
        tile_block = jnp.take(flow_state, wrapped, axis=2)
        temp_rows = jnp.take(surf_temp, wrapped, axis=0)
        blow_rows = jnp.take(surf_blow, wrapped, axis=0)
        kind_rows = jnp.take(bc_kind, wrapped, axis=0)
        ghost_one = wall_ghost(tile_block[:, 0], temp_rows, blow_rows, kind_rows)
        ghost_two = wall_ghost(tile_block[:, 1], temp_rows, blow_rows, kind_rows)
        far_rows = jnp.broadcast_to(jnp.array(far_values, jnp.float32)[:, None, None, None], (5, 2, CI + 4, NJ))
        padded_state = jnp.concatenate([ghost_two[:, None], ghost_one[:, None], tile_block, far_rows], axis=1)
        heights_block = lax.dynamic_slice_in_dim(shifted, first_row, CI, axis=1)
        norm_block = lax.dynamic_slice_in_dim(normalized, first_row, CI, axis=1)
        return advance(padded_state, extend_heights(heights_block), norm_block)

    blocks = lax.map(one_tile, jnp.arange(N_SURF, dtype=jnp.int32))
    state_next = jnp.moveaxis(blocks, 0, 2).reshape(5, NK, NI, NJ)
    return state_next, node_shift, ablator_next
```

```python
import functools

import jax
import jax.numpy as jnp
from jax import lax
from jax.experimental import pallas as pl
from jax.experimental.pallas import tpu as pltpu
from jax.sharding import PartitionSpec as P

f32 = jnp.float32
bf16 = jnp.bfloat16
MESH = pl.DeviceIdType.MESH

time_step = 0.15
viscosity = 0.05
conduction = 0.07
sponge_rate = 0.5
far_values = (1.0, 0.5, 0.0, 0.0, 2.625)
SCALE = time_step / 12.0
CHUNK = 4


def parts3(x):
    a = x.astype(bf16).astype(f32)
    b = (x - a).astype(bf16).astype(f32)
    c = (x - a - b).astype(bf16).astype(f32)
    return a, b, c


def shift_of(n):
    assert n & (n - 1) == 0
    return n.bit_length() - 1


def pick(index, table_ref, count):
    out = jnp.zeros(index.shape, f32)
    for z in range(count):
        out = jnp.where(index == z, table_ref[z], out)
    return out


def normal_fields(density, vx, vy, vz, pressure):
    energy = 2.5 * pressure + 0.5 * density * (vx * vx + vy * vy + vz * vz)
    svz = SCALE * vz
    rho_w = density * svz
    flux = (
        rho_w,
        rho_w * vx,
        rho_w * vy,
        rho_w * vz + SCALE * pressure,
        (energy + pressure) * svz,
    )
    cv = SCALE * viscosity
    return flux, (cv * vx, cv * vy, cv * vz, (SCALE * conduction) * (pressure / density))


def primitives_of(u0, u1, u2, u3, u4):
    inv = 1.0 / u0
    vx, vy, vz = u1 * inv, u2 * inv, u3 * inv
    pressure = 0.4 * (u4 - 0.5 * (u1 * vx + u2 * vy + u3 * vz))
    return inv, vx, vy, vz, pressure


def kernel(
    dims,
    flow, spacing, kind, cells, zones, abl, conduct, diffuse, rate,
    out, shift_out, abl_out,
    F3, Q, XR, XL, RL, RR, PM, V, send_list, recv_list, reply, reply_in,
    slab_total, totals_in, film_buf, film_in, part, part_in,
    halo_u, halo_s, sp, dense,
    s_list, r_list, s_rep, r_rep, s_tot, r_tot, s_film, r_film, s_part, r_part,
    s_hu, r_hu, s_hs, r_hs, s_x, r_x,
):
    K, I, J, NT, W, C, PT, NZ = dims
    R = I * J // 128
    JB = J // 128
    s = lax.axis_index("surf")
    w = lax.axis_index("wall")
    barrier = pltpu.get_barrier_semaphore()
    for d in range(1, NT):
        pl.semaphore_signal(barrier, inc=1, device_id=(lax.rem(s + d, NT), w), device_id_type=MESH)
    for d in range(1, W):
        pl.semaphore_signal(barrier, inc=1, device_id=(s, lax.rem(w + d, W)), device_id_type=MESH)

    def add_total(k, total):
        layer = spacing[k]
        sp[k + 2] = layer
        return total + layer

    slab_total[...] = lax.fori_loop(0, K, add_total, jnp.zeros((I, J), f32))
    inv, vx, vy, vz, pressure = primitives_of(*[flow[e, 0] for e in range(5)])
    film_buf[0] = 2.0 / spacing[0]
    film_buf[1] = pressure * inv + 0.2 * (vx * vx + vy * vy + vz * vz)

    cell = cells[...]
    tile = lax.shift_right_logical(cell, shift_of(I * J))
    within = jnp.bitwise_and(cell, I * J - 1)
    row_i = lax.shift_right_logical(within, shift_of(J))
    col_j = jnp.bitwise_and(within, J - 1)
    row = lax.shift_right_logical(col_j, 7) * I + row_i
    lane = jnp.bitwise_and(col_j, 127)
    zone = zones[...]
    tile_iota = lax.broadcasted_iota(jnp.int32, (NT, C), 0)
    lane_iota = lax.broadcasted_iota(jnp.int32, (NT, C), 1)
    mine = jnp.where(tile_iota == tile, 1.0, 0.0).astype(f32)
    run = mine
    step = 1
    while step < C:
        run = run + jnp.where(lane_iota >= step, pltpu.roll(run, step, 1), 0.0)
        step *= 2
    rank = jnp.sum(mine * run, axis=0, keepdims=True).astype(jnp.int32) - 1
    slot = tile * PT + rank
    V[...] = jnp.zeros(V.shape, f32)
    V[0:1, 0:C] = row.astype(f32)
    V[1:2, 0:C] = lane.astype(f32)
    V[2:3, 0:C] = zone.astype(f32)
    for n, piece in enumerate(parts3(abl[0:1, :]) + parts3(abl[1:2, :])):
        V[3 + n : 4 + n, 0:C] = piece
    payload = V[:, 0:C].astype(bf16)
    slot_iota = lax.broadcasted_iota(jnp.int32, (PT, C), 0)
    for t in range(NT):
        block = jnp.where(slot_iota + t * PT == slot, 1.0, 0.0).astype(bf16)
        PM[t * PT : (t + 1) * PT, :] = block
        got = lax.dot_general(payload, block, (((1,), (1,)), ((), ())), preferred_element_type=f32)
        send_list[t] = jnp.zeros((8, PT), f32)
        send_list[t, 0:3] = got[0:3]
        send_list[t, 3:4] = got[3:4] + got[4:5] + got[5:6]
        send_list[t, 4:5] = got[6:7] + got[7:8] + got[8:9]

    pl.semaphore_wait(barrier, NT - 1 + W - 1)

    def list_copy(d):
        t = lax.rem(s + d, NT)
        return pltpu.make_async_remote_copy(
            send_list.at[t], recv_list.at[d], s_list.at[d], r_list.at[d],
            device_id=(t, w), device_id_type=MESH)

    def total_copy(d):
        return pltpu.make_async_remote_copy(
            slab_total, totals_in.at[w], s_tot.at[d], r_tot.at[d],
            device_id=(s, lax.rem(w + d, W)), device_id_type=MESH)

    def film_copy(d):
        return pltpu.make_async_remote_copy(
            film_buf, film_in, s_film.at[d], r_film,
            device_id=(s, lax.rem(w + d, W)), device_id_type=MESH)

    def halo_copies(side):
        near, target = (K - 2, lax.rem(w + 1, W)) if side == 0 else (0, lax.rem(w + W - 1, W))
        return (
            pltpu.make_async_remote_copy(
                flow.at[:, near : near + 2], halo_u.at[side], s_hu.at[side], r_hu.at[side],
                device_id=(s, target), device_id_type=MESH),
            pltpu.make_async_remote_copy(
                spacing.at[near : near + 2], halo_s.at[side], s_hs.at[side], r_hs.at[side],
                device_id=(s, target), device_id_type=MESH),
        )

    for d in range(1, NT):
        list_copy(d).start()

    @pl.when(w == 0)
    def _():
        for d in range(1, W):
            film_copy(d).start()

    for d in range(1, W):
        total_copy(d).start()
    totals_in[w] = slab_total[...]

    @pl.when(w < W - 1)
    def _():
        for copy in halo_copies(0):
            copy.start()

    @pl.when(w > 0)
    def _():
        for copy in halo_copies(1):
            copy.start()

    def side_copies(c):
        ks = pl.ds(c * CHUNK, CHUNK)
        return (
            pltpu.make_async_remote_copy(
                XR.at[ks], RL.at[ks], s_x.at[0, c], r_x.at[0, c],
                device_id=(lax.rem(s + 1, NT), w), device_id_type=MESH),
            pltpu.make_async_remote_copy(
                XL.at[ks], RR.at[ks], s_x.at[1, c], r_x.at[1, c],
                device_id=(lax.rem(s + NT - 1, NT), w), device_id_type=MESH),
        )

    i_row = lax.broadcasted_iota(jnp.int32, (I, J), 0)

    def surface_terms(k, carry):
        u = [flow[e, k] for e in range(5)]
        inv, vx, vy, vz, pressure = primitives_of(*u)
        enthalpy = u[4] + pressure
        sx, sy, sz, sp_ = SCALE * vx, SCALE * vy, SCALE * vz, SCALE * pressure
        m12, m13, m23 = u[1] * sy, u[1] * sz, u[2] * sz
        q = (viscosity * sx, viscosity * sy, viscosity * sz,
             (conduction * inv) * sp_)
        f1 = (SCALE * u[1], u[1] * sx + sp_, m12, m13, enthalpy * sx)
        f2 = (SCALE * u[2], m12, u[2] * sy + sp_, m23, enthalpy * sy)
        f3 = (SCALE * u[3], m13, m23, u[3] * sz + sp_, enthalpy * sz)
        for e in range(5):
            F3[k + 2, e] = f3[e]
        for e in range(4):
            Q[k + 2, e] = q[e]
        for e in range(5):
            total = u[e]
            if e:
                qe = q[e - 1]
                total = total - 60.0 * qe
                q8 = 8.0 * qe
            for axis, size, flux in ((0, I, f1[e]), (1, J, f2[e])):
                if e:
                    up2 = flux - qe
                    down2 = -flux - qe
                    up1 = q8 - 8.0 * up2
                    down1 = q8 - 8.0 * down2
                else:
                    up2 = flux
                    down2 = -flux
                    up1 = -8.0 * flux
                    down1 = 8.0 * flux
                r1 = pltpu.roll(down1, 1, axis)
                r2 = pltpu.roll(down2, 2, axis)
                l1 = pltpu.roll(up1, size - 1, axis)
                l2 = pltpu.roll(up2, size - 2, axis)
                if axis == 0:
                    to_right = r2 + jnp.where(i_row == 0, r1, 0.0)
                    to_left = up2 + jnp.where(i_row == 1, pltpu.roll(up1, 1, 0), 0.0)
                    XR[k, e] = to_right[0:2]
                    XL[k, e] = to_left[0:2]
                    r1 = jnp.where(i_row >= 1, r1, 0.0)
                    r2 = jnp.where(i_row >= 2, r2, 0.0)
                    l1 = jnp.where(i_row <= I - 2, l1, 0.0)
                    l2 = jnp.where(i_row <= I - 3, l2, 0.0)
                total = total + ((r1 + r2) + (l1 + l2))
            out[e, k] = total
        return carry

    for c in range(K // CHUNK):
        lax.fori_loop(c * CHUNK, (c + 1) * CHUNK, surface_terms, 0)
        for copy in side_copies(c):
            copy.start()

    recv_list[0] = send_list[s]
    for d in range(1, NT):
        list_copy(d).wait()
    listed = jnp.concatenate([recv_list[d] for d in range(NT)], axis=1)
    count = NT * PT
    l_row = listed[0:1].astype(jnp.int32)
    l_lane = listed[1:2].astype(jnp.int32)
    row_hot = jnp.where(lax.broadcasted_iota(jnp.int32, (R, count), 0) == l_row, 1.0, 0.0)
    lane_hot = jnp.where(
        lax.broadcasted_iota(jnp.int32, (128, count), 0) == l_lane, 1.0, 0.0).astype(bf16)
    pieces = parts3(listed[3:4]) + parts3(listed[4:5]) + (listed[2:3],)
    stack = jnp.concatenate([row_hot * piece for piece in pieces], axis=0).astype(bf16)
    grid = lax.dot_general(stack, lane_hot, (((1,), (1,)), ((), ())), preferred_element_type=f32)
    first = grid[0:R] + grid[R : 2 * R] + grid[2 * R : 3 * R]
    second = grid[3 * R : 4 * R] + grid[4 * R : 5 * R] + grid[5 * R : 6 * R]
    zone_grid = grid[6 * R : 7 * R]

    @pl.when(w == 0)
    def _():
        for d in range(1, W):
            film_copy(d).wait_send()
        film_in[...] = film_buf[...]

    @pl.when(w > 0)
    def _():
        film_copy(1).wait_recv()

    film = jnp.concatenate([film_in[0, :, b * 128 : (b + 1) * 128] for b in range(JB)], axis=0)
    recov = jnp.concatenate([film_in[1, :, b * 128 : (b + 1) * 128] for b in range(JB)], axis=0)
    zone_grid = zone_grid.astype(jnp.int32)
    owned = first > 0.25
    cond = pick(zone_grid, conduct, NZ)
    surface = jnp.where(owned, first, 1.0)
    for newton_pass in range(2):
        cube = surface * surface * surface
        surface = (film * recov + cond * second + 2.4 * cube * surface) / (film + cond + 3.2 * cube)
    recess = pick(zone_grid, rate, NZ) * jnp.exp(-2.0 / surface)
    part[0] = jnp.where(owned, surface, 0.0)
    part[1] = jnp.where(owned, recess, 0.0)

    def part_copy(d):
        return pltpu.make_async_remote_copy(
            part, part_in.at[d], s_part.at[d], r_part.at[d],
            device_id=(s, lax.rem(w + d, W)), device_id_type=MESH)

    for d in range(1, W):
        part_copy(d).start()

    table = jnp.concatenate(parts3(part[0]), axis=0).astype(bf16)
    spread = jnp.dot(table, lane_hot, preferred_element_type=f32)
    spread = spread[0:R] + spread[R : 2 * R] + spread[2 * R : 3 * R]
    answer = jnp.sum(spread * row_hot, axis=0, keepdims=True)
    for d in range(NT):
        reply[d] = jnp.broadcast_to(answer[:, d * PT : (d + 1) * PT], (8, PT))

    def reply_copy(d):
        return pltpu.make_async_remote_copy(
            reply.at[d], reply_in.at[s], s_rep.at[d], r_rep.at[d],
            device_id=(lax.rem(s + NT - d, NT), w), device_id_type=MESH)

    for d in range(1, NT):
        reply_copy(d).start()
    reply_in[s] = reply[0]

    for d in range(1, W):
        part_copy(d).wait()
    whole = part[...]
    for d in range(1, W):
        whole = whole + part_in[d]
    dense[...] = whole
    surf_temp = jnp.concatenate([dense[0, b * I : (b + 1) * I, :] for b in range(JB)], axis=1)
    surf_recess = jnp.concatenate([dense[1, b * I : (b + 1) * I, :] for b in range(JB)], axis=1)

    for d in range(1, W):
        total_copy(d).wait()
    column_total = jnp.zeros((I, J), f32)
    offset = jnp.zeros((I, J), f32)
    for n in range(W):
        column_total = column_total + totals_in[n]
        offset = offset + jnp.where(n < w, totals_in[n], 0.0)

    @pl.when(w < W - 1)
    def _():
        for copy in halo_copies(0):
            copy.wait_send()
        for copy in halo_copies(1):
            copy.wait_recv()

    @pl.when(w > 0)
    def _():
        for copy in halo_copies(1):
            copy.wait_send()
        for copy in halo_copies(0):
            copy.wait_recv()

    def put(at, values):
        flux, fields = values
        for e in range(5):
            F3[at, e] = flux[e]
        for e in range(4):
            Q[at, e] = fields[e]

    def put_halo(side, base):
        for n in range(2):
            u = [halo_u[side, e, n] for e in range(5)]
            inv, vx, vy, vz, pressure = primitives_of(*u)
            put(base + n, normal_fields(u[0], vx, vy, vz, pressure))
            sp[base + n] = halo_s[side, n]

    @pl.when(w > 0)
    def _():
        put_halo(0, 0)

    @pl.when(w < W - 1)
    def _():
        put_halo(1, K + 2)

    @pl.when(w == 0)
    def _():
        kinds = kind[...]
        slip = kinds == 1
        for n in range(2):
            u = [flow[e, n] for e in range(5)]
            inv, vx, vy, vz, pressure = primitives_of(*u)
            density = jnp.where(slip, u[0], pressure / surf_temp)
            vx = jnp.where(slip, vx, -vx)
            vy = jnp.where(slip, vy, -vy)
            vz = jnp.where(kinds == 2, 2.0 * surf_recess - vz, -vz)
            put(1 - n, normal_fields(density, vx, vy, vz, pressure))
        sp[1] = spacing[1]
        sp[0] = spacing[0]

    @pl.when(w == W - 1)
    def _():
        one = jnp.full((I, J), 1.0, f32)
        zero = jnp.zeros((I, J), f32)
        for n in range(2):
            put(K + 2 + n, normal_fields(one, 0.5 * one, zero, zero, one))
        sp[K + 2] = spacing[K - 2]
        sp[K + 3] = spacing[K - 1]

    inv_total = 1.0 / column_total
    stretch = (1.0 + surf_recess * inv_total) * (1.0 / 12.0)

    def normal_terms(k, run):
        here = sp[k + 2]
        metric = stretch * (
            3.0 * (sp[k + 1] + sp[k + 3]) + 7.0 * here - 0.5 * (sp[k] + sp[k + 4]))
        inv_metric = 1.0 / metric
        inv_square = inv_metric * inv_metric
        normalized = (run + 0.5 * here) * inv_total
        shift_out[k] = surf_recess * (normalized - 1.0)
        damp = (time_step * sponge_rate) * normalized * normalized
        for e in range(5):
            diff = 8.0 * (F3[k + 3, e] - F3[k + 1, e]) - (F3[k + 4, e] - F3[k, e])
            total = out[e, k] - inv_metric * diff - damp * (flow[e, k] - far_values[e])
            if e:
                lap = (16.0 * (Q[k + 3, e - 1] + Q[k + 1, e - 1])
                       - (Q[k + 4, e - 1] + Q[k, e - 1]) - 30.0 * Q[k + 2, e - 1])
                total = total + inv_square * lap
            out[e, k] = total
        return run + here

    lax.fori_loop(0, K, normal_terms, offset)

    for d in range(1, NT):
        reply_copy(d).wait()
    answer = jnp.concatenate([reply_in[t, 0:1] for t in range(NT)], axis=1)
    V[...] = jnp.zeros(V.shape, f32)
    for n, piece in enumerate(parts3(answer)):
        V[n : n + 1, 0:count] = piece
    back = jnp.dot(V[:, 0:count].astype(bf16), PM[...], preferred_element_type=f32)
    col_surface = back[0:1] + back[1:2] + back[2:3]
    col_diffuse = pick(zone, diffuse, NZ)
    depth = abl.shape[0]
    depth_row = lax.broadcasted_iota(jnp.int32, (depth, C), 0)
    profile = jnp.where(depth_row == 0, col_surface, abl[...])
    for heat_pass in range(2):
        below = pltpu.roll(profile, 1, 0)
        above = jnp.where(depth_row == depth - 1, below, pltpu.roll(profile, depth - 1, 0))
        gain = col_diffuse * (above - 2.0 * profile + below)
        profile = jnp.where(depth_row == 0, profile, profile + gain)
    abl_out[...] = profile

    def add_sides(k, carry):
        for e in range(5):
            out[e, k, 0:2] = out[e, k, 0:2] + RL[k, e]
            out[e, k, I - 2 : I] = out[e, k, I - 2 : I] + RR[k, e]
        return carry

    for c in range(K // CHUNK):
        for copy in side_copies(c):
            copy.wait()
        lax.fori_loop(c * CHUNK, (c + 1) * CHUNK, add_sides, 0)


def shards(flow_state, spacing, bc_kind, cell_of, zone_id, abl_temp, conduct, diffuse, rate):
    NT = lax.axis_size("surf")
    W = lax.axis_size("wall")
    K, I, J = spacing.shape
    C = cell_of.shape[0]
    PT = -(-(C // NT) // 128) * 128
    R = I * J // 128
    count = NT * PT
    dims = (K, I, J, NT, W, C, PT, conduct.shape[0])
    vmem = pl.BlockSpec(memory_space=pltpu.VMEM)
    smem = pl.BlockSpec(memory_space=pltpu.SMEM)
    dma = pltpu.SemaphoreType.DMA
    chunks = K // CHUNK
    scratch = [
        pltpu.VMEM((K + 4, 5, I, J), f32),
        pltpu.VMEM((K + 4, 4, I, J), f32),
        pltpu.VMEM((K, 5, 2, J), f32),
        pltpu.VMEM((K, 5, 2, J), f32),
        pltpu.VMEM((K, 5, 2, J), f32),
        pltpu.VMEM((K, 5, 2, J), f32),
        pltpu.VMEM((count, C), bf16),
        pltpu.VMEM((16, max(C, count)), f32),
        pltpu.VMEM((NT, 8, PT), f32),
        pltpu.VMEM((NT, 8, PT), f32),
        pltpu.VMEM((NT, 8, PT), f32),
        pltpu.VMEM((NT, 8, PT), f32),
        pltpu.VMEM((I, J), f32),
        pltpu.VMEM((W, I, J), f32),
        pltpu.VMEM((2, I, J), f32),
        pltpu.VMEM((2, I, J), f32),
        pltpu.VMEM((2, R, 128), f32),
        pltpu.VMEM((W, 2, R, 128), f32),
        pltpu.VMEM((2, 5, 2, I, J), f32),
        pltpu.VMEM((2, 2, I, J), f32),
        pltpu.VMEM((K + 4, I, J), f32),
        pltpu.VMEM((2, R, 128), f32),
        dma((NT,)), dma((NT,)), dma((NT,)), dma((NT,)),
        dma((W,)), dma((W,)), dma((W,)), dma,
        dma((W,)), dma((W,)),
        dma((2,)), dma((2,)), dma((2,)), dma((2,)),
        dma((2, chunks)), dma((2, chunks)),
    ]
    return pl.pallas_call(
        functools.partial(kernel, dims),
        out_shape=(
            jax.ShapeDtypeStruct(flow_state.shape, f32),
            jax.ShapeDtypeStruct(spacing.shape, f32),
            jax.ShapeDtypeStruct(abl_temp.shape, f32),
        ),
        in_specs=[vmem] * 6 + [smem] * 3,
        out_specs=(vmem,) * 3,
        scratch_shapes=scratch,
        compiler_params=pltpu.CompilerParams(
            collective_id=0, has_side_effects=True, vmem_limit_bytes=50 * 1024 * 1024),
    )(flow_state, spacing, bc_kind, cell_of.reshape(1, C), zone_id.reshape(1, C), abl_temp,
      conduct, diffuse, rate)


def solution(mesh):
    in_specs = (
        P(None, "wall", "surf", None),
        P("wall", "surf", None),
        P("surf", None),
        P(("surf", "wall")),
        P(("surf", "wall")),
        P(None, ("surf", "wall")),
        P(),
        P(),
        P(),
    )
    out_specs = (P(None, "wall", "surf", None), P("wall", "surf", None), P(None, ("surf", "wall")))
    return jax.shard_map(shards, mesh=mesh, in_specs=in_specs, out_specs=out_specs, check_vma=False)
```

```python
import functools

import jax
import jax.numpy as jnp
from jax import lax
from jax.experimental import pallas as pl
from jax.experimental.pallas import tpu as pltpu
from jax.sharding import PartitionSpec as P

f32 = jnp.float32
bf16 = jnp.bfloat16
MESH = pl.DeviceIdType.MESH

time_step = 0.15
viscosity = 0.05
conduction = 0.07
sponge_rate = 0.5
far_values = (1.0, 0.5, 0.0, 0.0, 2.625)
SCALE = time_step / 12.0
CHUNK = 4
VMEM_BYTES = 62 * 1024 * 1024
PIECES = 2


def parts3(x):
    a = x.astype(bf16).astype(f32)
    b = (x - a).astype(bf16).astype(f32)
    c = (x - a - b).astype(bf16).astype(f32)
    return a, b, c


def shift_of(n):
    assert n & (n - 1) == 0
    return n.bit_length() - 1


def pick(index, table_ref, count):
    out = jnp.zeros(index.shape, f32)
    for z in range(count):
        out = jnp.where(index == z, table_ref[z], out)
    return out


def normal_fields(density, vx, vy, vz, pressure):
    energy = 2.5 * pressure + 0.5 * density * (vx * vx + vy * vy + vz * vz)
    svz = SCALE * vz
    rho_w = density * svz
    flux = (
        rho_w,
        rho_w * vx,
        rho_w * vy,
        rho_w * vz + SCALE * pressure,
        (energy + pressure) * svz,
    )
    cv = SCALE * viscosity
    return flux, (cv * vx, cv * vy, cv * vz, (SCALE * conduction) * (pressure / density))


def primitives_of(u0, u1, u2, u3, u4):
    inv = 1.0 / u0
    vx, vy, vz = u1 * inv, u2 * inv, u3 * inv
    pressure = 0.4 * (u4 - 0.5 * (u1 * vx + u2 * vy + u3 * vz))
    return inv, vx, vy, vz, pressure


def kernel(
    dims,
    flow_hbm, spacing_hbm, kind_hbm, cells_hbm, zones_hbm, abl_hbm, conduct_hbm, diffuse_hbm, rate_hbm,
    out_hbm, shift_hbm, abl_out_hbm,
    out, shift_out, abl_out, s_out,
    flow, spacing, kind, cells, zones, abl, conduct, diffuse, rate, s_flow, s_in,
    F3, Q, XR, XL, RL, RR, PM, V, send_list, recv_list, reply, reply_in,
    slab_total, totals_in, film_buf, film_in, part, part_in,
    halo_u, halo_s, sp, dense,
    s_list, r_list, s_rep, r_rep, s_tot, r_tot, s_film, r_film, s_part, r_part,
    s_hu, r_hu, s_hs, r_hs, s_x, r_x,
):
    K, I, J, NT, W, C, PT, NZ = dims
    R = I * J // 128
    JB = J // 128
    s = lax.axis_index("surf")
    w = lax.axis_index("wall")

    def flow_copy(c):
        ks = pl.ds(c * CHUNK, CHUNK)
        return pltpu.make_async_copy(flow_hbm.at[:, ks], flow.at[:, ks], s_flow.at[c])

    pairs = ((spacing_hbm, spacing), (cells_hbm, cells), (zones_hbm, zones), (abl_hbm, abl),
             (kind_hbm, kind), (conduct_hbm, conduct), (diffuse_hbm, diffuse), (rate_hbm, rate))
    inputs = [pltpu.make_async_copy(a, b, s_in.at[n]) for n, (a, b) in enumerate(pairs)]
    flow_copy(0).start()
    for copy in inputs:
        copy.start()
    for c in range(1, K // CHUNK):
        flow_copy(c).start()
    barrier = pltpu.get_barrier_semaphore()
    for d in range(1, NT):
        pl.semaphore_signal(barrier, inc=1, device_id=(lax.rem(s + d, NT), w), device_id_type=MESH)
    for d in range(1, W):
        pl.semaphore_signal(barrier, inc=1, device_id=(s, lax.rem(w + d, W)), device_id_type=MESH)

    def list_copy(d):
        t = lax.rem(s + d, NT)
        return pltpu.make_async_remote_copy(
            send_list.at[t], recv_list.at[d], s_list.at[d], r_list.at[d],
            device_id=(t, w), device_id_type=MESH)

    def total_copy(d):
        return pltpu.make_async_remote_copy(
            slab_total, totals_in.at[w], s_tot.at[d], r_tot.at[d],
            device_id=(s, lax.rem(w + d, W)), device_id_type=MESH)

    def film_copy(d):
        return pltpu.make_async_remote_copy(
            film_buf, film_in, s_film.at[d], r_film,
            device_id=(s, lax.rem(w + d, W)), device_id_type=MESH)

    def halo_copies(side):
        near, target = (K - 2, lax.rem(w + 1, W)) if side == 0 else (0, lax.rem(w + W - 1, W))
        return (
            pltpu.make_async_remote_copy(
                flow_hbm.at[:, near : near + 2], halo_u.at[side], s_hu.at[side], r_hu.at[side],
                device_id=(s, target), device_id_type=MESH),
            pltpu.make_async_remote_copy(
                spacing_hbm.at[near : near + 2], halo_s.at[side], s_hs.at[side], r_hs.at[side],
                device_id=(s, target), device_id_type=MESH),
        )

    def side_copies(c):
        ks = pl.ds(c * CHUNK, CHUNK)
        return (
            pltpu.make_async_remote_copy(
                XR.at[ks], RL.at[ks], s_x.at[0, c], r_x.at[0, c],
                device_id=(lax.rem(s + 1, NT), w), device_id_type=MESH),
            pltpu.make_async_remote_copy(
                XL.at[ks], RR.at[ks], s_x.at[1, c], r_x.at[1, c],
                device_id=(lax.rem(s + NT - 1, NT), w), device_id_type=MESH),
        )

    i_row = lax.broadcasted_iota(jnp.int32, (I, J), 0)

    def surface_terms(k, carry):
        u = [flow[e, k] for e in range(5)]
        inv, vx, vy, vz, pressure = primitives_of(*u)
        enthalpy = u[4] + pressure
        sx, sy, sz, sp_ = SCALE * vx, SCALE * vy, SCALE * vz, SCALE * pressure
        m12, m13, m23 = u[1] * sy, u[1] * sz, u[2] * sz
        q = (viscosity * sx, viscosity * sy, viscosity * sz,
             (conduction * inv) * sp_)
        f1 = (SCALE * u[1], u[1] * sx + sp_, m12, m13, enthalpy * sx)
        f2 = (SCALE * u[2], m12, u[2] * sy + sp_, m23, enthalpy * sy)
        f3 = (SCALE * u[3], m13, m23, u[3] * sz + sp_, enthalpy * sz)
        for e in range(5):
            F3[k + 2, e] = f3[e]
        for e in range(4):
            Q[k + 2, e] = q[e]
        for e in range(5):
            total = u[e]
            if e:
                qe = q[e - 1]
                total = total - 60.0 * qe
                q8 = 8.0 * qe
            for axis, size, flux in ((0, I, f1[e]), (1, J, f2[e])):
                if e:
                    up2 = flux - qe
                    down2 = -flux - qe
                    up1 = q8 - 8.0 * up2
                    down1 = q8 - 8.0 * down2
                else:
                    up2 = flux
                    down2 = -flux
                    up1 = -8.0 * flux
                    down1 = 8.0 * flux
                r1 = pltpu.roll(down1, 1, axis)
                r2 = pltpu.roll(down2, 2, axis)
                l1 = pltpu.roll(up1, size - 1, axis)
                l2 = pltpu.roll(up2, size - 2, axis)
                if axis == 0:
                    to_right = r2 + jnp.where(i_row == 0, r1, 0.0)
                    to_left = up2 + jnp.where(i_row == 1, pltpu.roll(up1, 1, 0), 0.0)
                    XR[k, e] = to_right[0:2]
                    XL[k, e] = to_left[0:2]
                    r1 = jnp.where(i_row >= 1, r1, 0.0)
                    r2 = jnp.where(i_row >= 2, r2, 0.0)
                    l1 = jnp.where(i_row <= I - 2, l1, 0.0)
                    l2 = jnp.where(i_row <= I - 3, l2, 0.0)
                total = total + ((r1 + r2) + (l1 + l2))
            out[e, k] = total
        return carry

    def chunk(c, send=True):
        flow_copy(c).wait()
        lax.fori_loop(c * CHUNK, (c + 1) * CHUNK, surface_terms, 0)
        if send:
            for copy in side_copies(c):
                copy.start()

    chunk(0, send=False)
    pl.semaphore_wait(barrier, NT - 1 + W - 1)
    for copy in side_copies(0):
        copy.start()
    @pl.when(w < W - 1)
    def _():
        for copy in halo_copies(0):
            copy.start()

    @pl.when(w > 0)
    def _():
        for copy in halo_copies(1):
            copy.start()

    chunk(1)
    inputs[0].wait()
    def add_total(k, total):
        layer = spacing[k]
        sp[k + 2] = layer
        return total + layer

    slab_total[...] = lax.fori_loop(0, K, add_total, jnp.zeros((I, J), f32))
    inv, vx, vy, vz, pressure = primitives_of(*[flow[e, 0] for e in range(5)])
    film_buf[0] = 2.0 / spacing[0]
    film_buf[1] = pressure * inv + 0.2 * (vx * vx + vy * vy + vz * vz)

    @pl.when(w == 0)
    def _():
        for d in range(1, W):
            film_copy(d).start()

    for d in range(1, W):
        total_copy(d).start()
    totals_in[w] = slab_total[...]

    chunk(2)

    for copy in inputs[1:]:
        copy.wait()
    cell = cells[...]
    tile = lax.shift_right_logical(cell, shift_of(I * J))
    within = jnp.bitwise_and(cell, I * J - 1)
    row_i = lax.shift_right_logical(within, shift_of(J))
    col_j = jnp.bitwise_and(within, J - 1)
    row = lax.shift_right_logical(col_j, 7) * I + row_i
    lane = jnp.bitwise_and(col_j, 127)
    zone = zones[...]
    tile_iota = lax.broadcasted_iota(jnp.int32, (NT, C), 0)
    lane_iota = lax.broadcasted_iota(jnp.int32, (NT, C), 1)
    mine = jnp.where(tile_iota == tile, 1.0, 0.0).astype(f32)
    run = mine
    step = 1
    while step < C:
        run = run + jnp.where(lane_iota >= step, pltpu.roll(run, step, 1), 0.0)
        step *= 2
    rank = jnp.sum(mine * run, axis=0, keepdims=True).astype(jnp.int32) - 1
    slot = tile * PT + rank
    V[...] = jnp.zeros(V.shape, f32)
    V[0:1, 0:C] = row.astype(f32)
    V[1:2, 0:C] = lane.astype(f32)
    V[2:3, 0:C] = zone.astype(f32)
    for n, piece in enumerate(parts3(abl[0:1, :]) + parts3(abl[1:2, :])):
        V[3 + n : 4 + n, 0:C] = piece
    payload = V[:, 0:C].astype(bf16)
    slot_iota = lax.broadcasted_iota(jnp.int32, (PT, C), 0)
    for t in range(NT):
        block = jnp.where(slot_iota + t * PT == slot, 1.0, 0.0).astype(bf16)
        PM[t * PT : (t + 1) * PT, :] = block
        got = lax.dot_general(payload, block, (((1,), (1,)), ((), ())), preferred_element_type=f32)
        send_list[t] = jnp.zeros((8, PT), f32)
        send_list[t, 0:3] = got[0:3]
        send_list[t, 3:4] = got[3:4] + got[4:5] + got[5:6]
        send_list[t, 4:5] = got[6:7] + got[7:8] + got[8:9]

    for d in range(1, NT):
        list_copy(d).start()

    for c in (3, 4, 5):
        chunk(c)

    recv_list[0] = send_list[s]
    for d in range(1, NT):
        list_copy(d).wait()
    listed = jnp.concatenate([recv_list[d] for d in range(NT)], axis=1)
    count = NT * PT
    l_row = listed[0:1].astype(jnp.int32)
    l_lane = listed[1:2].astype(jnp.int32)
    row_hot = jnp.where(lax.broadcasted_iota(jnp.int32, (R, count), 0) == l_row, 1.0, 0.0)
    lane_hot = jnp.where(
        lax.broadcasted_iota(jnp.int32, (128, count), 0) == l_lane, 1.0, 0.0).astype(bf16)
    pieces = parts3(listed[3:4]) + parts3(listed[4:5]) + (listed[2:3],)
    stack = jnp.concatenate([row_hot * piece for piece in pieces], axis=0).astype(bf16)
    grid = lax.dot_general(stack, lane_hot, (((1,), (1,)), ((), ())), preferred_element_type=f32)
    first = grid[0:R] + grid[R : 2 * R] + grid[2 * R : 3 * R]
    second = grid[3 * R : 4 * R] + grid[4 * R : 5 * R] + grid[5 * R : 6 * R]
    zone_grid = grid[6 * R : 7 * R]

    @pl.when(w == 0)
    def _():
        for d in range(1, W):
            film_copy(d).wait_send()
        film_in[...] = film_buf[...]

    @pl.when(w > 0)
    def _():
        film_copy(1).wait_recv()

    film = jnp.concatenate([film_in[0, :, b * 128 : (b + 1) * 128] for b in range(JB)], axis=0)
    recov = jnp.concatenate([film_in[1, :, b * 128 : (b + 1) * 128] for b in range(JB)], axis=0)
    zone_grid = zone_grid.astype(jnp.int32)
    owned = first > 0.25
    cond = pick(zone_grid, conduct, NZ)
    surface = jnp.where(owned, first, 1.0)
    for newton_pass in range(2):
        cube = surface * surface * surface
        surface = (film * recov + cond * second + 2.4 * cube * surface) / (film + cond + 3.2 * cube)
    recess = pick(zone_grid, rate, NZ) * jnp.exp(-2.0 / surface)
    part[0] = jnp.where(owned, surface, 0.0)
    part[1] = jnp.where(owned, recess, 0.0)

    def part_copy(d):
        return pltpu.make_async_remote_copy(
            part, part_in.at[d], s_part.at[d], r_part.at[d],
            device_id=(s, lax.rem(w + d, W)), device_id_type=MESH)

    for d in range(1, W):
        part_copy(d).start()

    table = jnp.concatenate(parts3(part[0]), axis=0).astype(bf16)
    spread = jnp.dot(table, lane_hot, preferred_element_type=f32)
    spread = spread[0:R] + spread[R : 2 * R] + spread[2 * R : 3 * R]
    answer = jnp.sum(spread * row_hot, axis=0, keepdims=True)
    for d in range(NT):
        reply[d] = jnp.broadcast_to(answer[:, d * PT : (d + 1) * PT], (8, PT))

    def reply_copy(d):
        return pltpu.make_async_remote_copy(
            reply.at[d], reply_in.at[s], s_rep.at[d], r_rep.at[d],
            device_id=(lax.rem(s + NT - d, NT), w), device_id_type=MESH)

    for d in range(1, NT):
        reply_copy(d).start()
    reply_in[s] = reply[0]
    for c in range(6, K // CHUNK):
        chunk(c)

    for d in range(1, W):
        part_copy(d).wait()
    whole = part[...]
    for d in range(1, W):
        whole = whole + part_in[d]
    dense[...] = whole
    surf_temp = jnp.concatenate([dense[0, b * I : (b + 1) * I, :] for b in range(JB)], axis=1)
    surf_recess = jnp.concatenate([dense[1, b * I : (b + 1) * I, :] for b in range(JB)], axis=1)

    for d in range(1, W):
        total_copy(d).wait()
    column_total = jnp.zeros((I, J), f32)
    offset = jnp.zeros((I, J), f32)
    for n in range(W):
        column_total = column_total + totals_in[n]
        offset = offset + jnp.where(n < w, totals_in[n], 0.0)

    @pl.when(w < W - 1)
    def _():
        for copy in halo_copies(0):
            copy.wait_send()
        for copy in halo_copies(1):
            copy.wait_recv()

    @pl.when(w > 0)
    def _():
        for copy in halo_copies(1):
            copy.wait_send()
        for copy in halo_copies(0):
            copy.wait_recv()

    def put(at, values):
        flux, fields = values
        for e in range(5):
            F3[at, e] = flux[e]
        for e in range(4):
            Q[at, e] = fields[e]

    def put_halo(side, base):
        for n in range(2):
            u = [halo_u[side, e, n] for e in range(5)]
            inv, vx, vy, vz, pressure = primitives_of(*u)
            put(base + n, normal_fields(u[0], vx, vy, vz, pressure))
            sp[base + n] = halo_s[side, n]

    @pl.when(w > 0)
    def _():
        put_halo(0, 0)

    @pl.when(w < W - 1)
    def _():
        put_halo(1, K + 2)

    @pl.when(w == 0)
    def _():
        kinds = kind[...]
        slip = kinds == 1
        for n in range(2):
            u = [flow[e, n] for e in range(5)]
            inv, vx, vy, vz, pressure = primitives_of(*u)
            density = jnp.where(slip, u[0], pressure / surf_temp)
            vx = jnp.where(slip, vx, -vx)
            vy = jnp.where(slip, vy, -vy)
            vz = jnp.where(kinds == 2, 2.0 * surf_recess - vz, -vz)
            put(1 - n, normal_fields(density, vx, vy, vz, pressure))
        sp[1] = spacing[1]
        sp[0] = spacing[0]

    @pl.when(w == W - 1)
    def _():
        one = jnp.full((I, J), 1.0, f32)
        zero = jnp.zeros((I, J), f32)
        for n in range(2):
            put(K + 2 + n, normal_fields(one, 0.5 * one, zero, zero, one))
        sp[K + 2] = spacing[K - 2]
        sp[K + 3] = spacing[K - 1]

    inv_total = 1.0 / column_total
    stretch = (1.0 + surf_recess * inv_total) * (1.0 / 12.0)

    def normal_terms(k, run):
        here = sp[k + 2]
        metric = stretch * (
            3.0 * (sp[k + 1] + sp[k + 3]) + 7.0 * here - 0.5 * (sp[k] + sp[k + 4]))
        inv_metric = 1.0 / metric
        inv_square = inv_metric * inv_metric
        normalized = (run + 0.5 * here) * inv_total
        shift_out[k] = surf_recess * (normalized - 1.0)
        damp = (time_step * sponge_rate) * normalized * normalized
        for e in range(5):
            diff = 8.0 * (F3[k + 3, e] - F3[k + 1, e]) - (F3[k + 4, e] - F3[k, e])
            total = out[e, k] - inv_metric * diff - damp * (flow[e, k] - far_values[e])
            if e:
                lap = (16.0 * (Q[k + 3, e - 1] + Q[k + 1, e - 1])
                       - (Q[k + 4, e - 1] + Q[k, e - 1]) - 30.0 * Q[k + 2, e - 1])
                total = total + inv_square * lap
            out[e, k] = total
        return run + here

    lax.fori_loop(0, K, normal_terms, offset)
    shift_copy = pltpu.make_async_copy(shift_out, shift_hbm, s_out.at[0])
    shift_copy.start()

    for d in range(1, NT):
        reply_copy(d).wait()
    answer = jnp.concatenate([reply_in[t, 0:1] for t in range(NT)], axis=1)
    V[...] = jnp.zeros(V.shape, f32)
    for n, piece in enumerate(parts3(answer)):
        V[n : n + 1, 0:count] = piece
    back = jnp.dot(V[:, 0:count].astype(bf16), PM[...], preferred_element_type=f32)
    col_surface = back[0:1] + back[1:2] + back[2:3]
    col_diffuse = pick(zone, diffuse, NZ)
    depth = abl.shape[0]
    depth_row = lax.broadcasted_iota(jnp.int32, (depth, C), 0)
    profile = jnp.where(depth_row == 0, col_surface, abl[...])
    for heat_pass in range(2):
        below = pltpu.roll(profile, 1, 0)
        above = jnp.where(depth_row == depth - 1, below, pltpu.roll(profile, depth - 1, 0))
        gain = col_diffuse * (above - 2.0 * profile + below)
        profile = jnp.where(depth_row == 0, profile, profile + gain)
    abl_out[...] = profile
    abl_copy = pltpu.make_async_copy(abl_out, abl_out_hbm, s_out.at[1])
    abl_copy.start()

    def add_sides(k, carry):
        for e in range(5):
            out[e, k, 0:2] = out[e, k, 0:2] + RL[k, e]
            out[e, k, I - 2 : I] = out[e, k, I - 2 : I] + RR[k, e]
        return carry

    def out_copy(c):
        ks = pl.ds(c * CHUNK, CHUNK)
        return pltpu.make_async_copy(out.at[:, ks], out_hbm.at[:, ks], s_out.at[2 + c])

    for c in range(K // CHUNK):
        for copy in side_copies(c):
            copy.wait()
        lax.fori_loop(c * CHUNK, (c + 1) * CHUNK, add_sides, 0)
        out_copy(c).start()
    shift_copy.wait()
    abl_copy.wait()
    for c in range(K // CHUNK):
        out_copy(c).wait()


def hand_out(a, b, c, to_a, to_b, to_c, sem):
    half = a.shape[1] // PIECES
    copies = [pltpu.make_async_copy(b, to_b, sem.at[0]), pltpu.make_async_copy(c, to_c, sem.at[1])]
    for e in range(a.shape[0]):
        for n in range(PIECES):
            ks = pl.ds(n * half, half)
            copies.append(pltpu.make_async_copy(a.at[e, ks], to_a.at[e, ks], sem.at[len(copies)]))
    for copy in copies:
        copy.start()
    for copy in copies:
        copy.wait()


def shards(flow_state, spacing, bc_kind, cell_of, zone_id, abl_temp, conduct, diffuse, rate):
    NT = lax.axis_size("surf")
    W = lax.axis_size("wall")
    K, I, J = spacing.shape
    C = cell_of.shape[0]
    PT = -(-(C // NT) // 128) * 128
    R = I * J // 128
    count = NT * PT
    dims = (K, I, J, NT, W, C, PT, conduct.shape[0])
    dma = pltpu.SemaphoreType.DMA
    chunks = K // CHUNK
    scratch = [
        pltpu.VMEM(flow_state.shape, f32),
        pltpu.VMEM(spacing.shape, f32),
        pltpu.VMEM(abl_temp.shape, f32),
        dma((chunks + 2,)),
        pltpu.VMEM(flow_state.shape, f32),
        pltpu.VMEM(spacing.shape, f32),
        pltpu.VMEM(bc_kind.shape, jnp.int32),
        pltpu.VMEM((1, C), jnp.int32),
        pltpu.VMEM((1, C), jnp.int32),
        pltpu.VMEM(abl_temp.shape, f32),
        pltpu.SMEM(conduct.shape, f32),
        pltpu.SMEM(conduct.shape, f32),
        pltpu.SMEM(conduct.shape, f32),
        dma((chunks,)), dma((8,)),
        pltpu.VMEM((K + 4, 5, I, J), f32),
        pltpu.VMEM((K + 4, 4, I, J), f32),
        pltpu.VMEM((K, 5, 2, J), f32),
        pltpu.VMEM((K, 5, 2, J), f32),
        pltpu.VMEM((K, 5, 2, J), f32),
        pltpu.VMEM((K, 5, 2, J), f32),
        pltpu.VMEM((count, C), bf16),
        pltpu.VMEM((16, max(C, count)), f32),
        pltpu.VMEM((NT, 8, PT), f32),
        pltpu.VMEM((NT, 8, PT), f32),
        pltpu.VMEM((NT, 8, PT), f32),
        pltpu.VMEM((NT, 8, PT), f32),
        pltpu.VMEM((I, J), f32),
        pltpu.VMEM((W, I, J), f32),
        pltpu.VMEM((2, I, J), f32),
        pltpu.VMEM((2, I, J), f32),
        pltpu.VMEM((2, R, 128), f32),
        pltpu.VMEM((W, 2, R, 128), f32),
        pltpu.VMEM((2, 5, 2, I, J), f32),
        pltpu.VMEM((2, 2, I, J), f32),
        pltpu.VMEM((K + 4, I, J), f32),
        pltpu.VMEM((2, R, 128), f32),
        dma((NT,)), dma((NT,)), dma((NT,)), dma((NT,)),
        dma((W,)), dma((W,)), dma((W,)), dma,
        dma((W,)), dma((W,)),
        dma((2,)), dma((2,)), dma((2,)), dma((2,)),
        dma((2, chunks)), dma((2, chunks)),
    ]
    hbm = pl.BlockSpec(memory_space=pltpu.HBM)
    results = pl.pallas_call(
        functools.partial(kernel, dims),
        out_shape=(
            jax.ShapeDtypeStruct(flow_state.shape, f32),
            jax.ShapeDtypeStruct(spacing.shape, f32),
            jax.ShapeDtypeStruct(abl_temp.shape, f32),
        ),
        in_specs=[hbm] * 9,
        out_specs=(hbm,) * 3,
        scratch_shapes=scratch,
        compiler_params=pltpu.CompilerParams(
            collective_id=0, has_side_effects=True, vmem_limit_bytes=VMEM_BYTES),
    )(flow_state, spacing, bc_kind, cell_of.reshape(1, C), zone_id.reshape(1, C), abl_temp,
      conduct, diffuse, rate)
    return pl.pallas_call(
        hand_out,
        out_shape=[jax.ShapeDtypeStruct(r.shape, f32) for r in results],
        in_specs=[hbm] * 3,
        out_specs=[hbm] * 3,
        scratch_shapes=[dma((2 + 5 * PIECES,))],
        compiler_params=pltpu.CompilerParams(vmem_limit_bytes=VMEM_BYTES),
    )(*results)


def solution(mesh):
    in_specs = (
        P(None, "wall", "surf", None),
        P("wall", "surf", None),
        P("surf", None),
        P(("surf", "wall")),
        P(("surf", "wall")),
        P(None, ("surf", "wall")),
        P(),
        P(),
        P(),
    )
    out_specs = (P(None, "wall", "surf", None), P("wall", "surf", None), P(None, ("surf", "wall")))
    return jax.shard_map(shards, mesh=mesh, in_specs=in_specs, out_specs=out_specs, check_vma=False)
```

```python
import functools

import jax
import jax.numpy as jnp
from jax import lax
from jax.experimental import pallas as pl
from jax.experimental.pallas import tpu as pltpu
from jax.sharding import PartitionSpec as P

f32 = jnp.float32
bf16 = jnp.bfloat16
MESH = pl.DeviceIdType.MESH

time_step = 0.15
viscosity = 0.05
conduction = 0.07
sponge_rate = 0.5
far_values = (1.0, 0.5, 0.0, 0.0, 2.625)
SCALE = time_step / 12.0
CHUNK = 4
HAND = 4
VMEM_BYTES = 62 * 1024 * 1024


def bounds_of(K):
    return (0, 2) + tuple(range(4, K + 1, CHUNK))


def parts3(x):
    a = x.astype(bf16).astype(f32)
    b = (x - a).astype(bf16).astype(f32)
    c = (x - a - b).astype(bf16).astype(f32)
    return a, b, c


def shift_of(n):
    assert n & (n - 1) == 0
    return n.bit_length() - 1


def pick(index, table_ref, count):
    out = jnp.zeros(index.shape, f32)
    for z in range(count):
        out = jnp.where(index == z, table_ref[z], out)
    return out


def normal_fields(density, vx, vy, vz, pressure):
    energy = 2.5 * pressure + 0.5 * density * (vx * vx + vy * vy + vz * vz)
    svz = SCALE * vz
    rho_w = density * svz
    flux = (
        rho_w,
        rho_w * vx,
        rho_w * vy,
        rho_w * vz + SCALE * pressure,
        (energy + pressure) * svz,
    )
    cv = SCALE * viscosity
    return flux, (cv * vx, cv * vy, cv * vz, (SCALE * conduction) * (pressure / density))


def primitives_of(u0, u1, u2, u3, u4):
    inv = 1.0 / u0
    vx, vy, vz = u1 * inv, u2 * inv, u3 * inv
    pressure = 0.4 * (u4 - 0.5 * (u1 * vx + u2 * vy + u3 * vz))
    return inv, vx, vy, vz, pressure


def kernel(
    dims,
    flow_hbm, spacing_hbm, kind_hbm, cells_hbm, zones_hbm, abl_hbm, conduct_hbm, diffuse_hbm, rate_hbm,
    out_hbm, shift_hbm, abl_out_hbm, RL, RR,
    out, shift_out, abl_out, s_out,
    flow, spacing, kind, cells, zones, abl, conduct, diffuse, rate, s_flow, s_in,
    F3, Q, XR, XL, PM, V, send_list, recv_list, reply, reply_in,
    slab_total, totals_in, film_buf, film_in, part, part_in,
    halo_u, halo_s, sp, dense,
    s_list, r_list, s_rep, r_rep, s_tot, r_tot, s_film, r_film, s_part, r_part,
    s_hu, r_hu, s_hs, r_hs, s_x, r_x,
):
    K, I, J, NT, W, C, PT, NZ = dims
    R = I * J // 128
    JB = J // 128
    s = lax.axis_index("surf")
    w = lax.axis_index("wall")

    cuts = bounds_of(K)
    chunks = len(cuts) - 1

    def flow_copy(c):
        ks = pl.ds(cuts[c], cuts[c + 1] - cuts[c])
        return pltpu.make_async_copy(flow_hbm.at[:, ks], flow.at[:, ks], s_flow.at[c])

    pairs = ((spacing_hbm, spacing), (cells_hbm, cells), (zones_hbm, zones), (abl_hbm, abl),
             (kind_hbm, kind), (conduct_hbm, conduct), (diffuse_hbm, diffuse), (rate_hbm, rate))
    inputs = [pltpu.make_async_copy(a, b, s_in.at[n]) for n, (a, b) in enumerate(pairs)]
    flow_copy(0).start()
    for copy in inputs:
        copy.start()
    for c in range(1, chunks):
        flow_copy(c).start()
    barrier = pltpu.get_barrier_semaphore()
    for d in range(1, NT):
        pl.semaphore_signal(barrier, inc=1, device_id=(lax.rem(s + d, NT), w), device_id_type=MESH)
    for d in range(1, W):
        pl.semaphore_signal(barrier, inc=1, device_id=(s, lax.rem(w + d, W)), device_id_type=MESH)

    def list_copy(d):
        t = lax.rem(s + d, NT)
        return pltpu.make_async_remote_copy(
            send_list.at[t], recv_list.at[d], s_list.at[d], r_list.at[d],
            device_id=(t, w), device_id_type=MESH)

    def total_copy(d):
        return pltpu.make_async_remote_copy(
            slab_total, totals_in.at[w], s_tot.at[d], r_tot.at[d],
            device_id=(s, lax.rem(w + d, W)), device_id_type=MESH)

    def film_copy(d):
        return pltpu.make_async_remote_copy(
            film_buf, film_in, s_film.at[d], r_film,
            device_id=(s, lax.rem(w + d, W)), device_id_type=MESH)

    def halo_copies(side):
        near, target = (K - 2, lax.rem(w + 1, W)) if side == 0 else (0, lax.rem(w + W - 1, W))
        return (
            pltpu.make_async_remote_copy(
                flow_hbm.at[:, near : near + 2], halo_u.at[side], s_hu.at[side], r_hu.at[side],
                device_id=(s, target), device_id_type=MESH),
            pltpu.make_async_remote_copy(
                spacing_hbm.at[near : near + 2], halo_s.at[side], s_hs.at[side], r_hs.at[side],
                device_id=(s, target), device_id_type=MESH),
        )

    def side_copies(c):
        ks = pl.ds(cuts[c], cuts[c + 1] - cuts[c])
        return (
            pltpu.make_async_remote_copy(
                XR.at[ks], RL.at[ks], s_x.at[0, c], r_x.at[0, c],
                device_id=(lax.rem(s + 1, NT), w), device_id_type=MESH),
            pltpu.make_async_remote_copy(
                XL.at[ks], RR.at[ks], s_x.at[1, c], r_x.at[1, c],
                device_id=(lax.rem(s + NT - 1, NT), w), device_id_type=MESH),
        )

    i_row = lax.broadcasted_iota(jnp.int32, (I, J), 0)

    def surface_terms(k, carry):
        u = [flow[e, k] for e in range(5)]
        inv, vx, vy, vz, pressure = primitives_of(*u)
        enthalpy = u[4] + pressure
        sx, sy, sz, sp_ = SCALE * vx, SCALE * vy, SCALE * vz, SCALE * pressure
        m12, m13, m23 = u[1] * sy, u[1] * sz, u[2] * sz
        q = (viscosity * sx, viscosity * sy, viscosity * sz,
             (conduction * inv) * sp_)
        f1 = (SCALE * u[1], u[1] * sx + sp_, m12, m13, enthalpy * sx)
        f2 = (SCALE * u[2], m12, u[2] * sy + sp_, m23, enthalpy * sy)
        f3 = (SCALE * u[3], m13, m23, u[3] * sz + sp_, enthalpy * sz)
        for e in range(5):
            F3[k + 2, e] = f3[e]
        for e in range(4):
            Q[k + 2, e] = q[e]
        for e in range(5):
            total = u[e]
            if e:
                qe = q[e - 1]
                total = total - 60.0 * qe
                q8 = 8.0 * qe
            for axis, size, flux in ((0, I, f1[e]), (1, J, f2[e])):
                if e:
                    up2 = flux - qe
                    down2 = -flux - qe
                    up1 = q8 - 8.0 * up2
                    down1 = q8 - 8.0 * down2
                else:
                    up2 = flux
                    down2 = -flux
                    up1 = -8.0 * flux
                    down1 = 8.0 * flux
                r1 = pltpu.roll(down1, 1, axis)
                r2 = pltpu.roll(down2, 2, axis)
                l1 = pltpu.roll(up1, size - 1, axis)
                l2 = pltpu.roll(up2, size - 2, axis)
                if axis == 0:
                    to_right = r2 + jnp.where(i_row == 0, r1, 0.0)
                    to_left = up2 + jnp.where(i_row == 1, pltpu.roll(up1, 1, 0), 0.0)
                    XR[k, e] = to_right[0:2]
                    XL[k, e] = to_left[0:2]
                    r1 = jnp.where(i_row >= 1, r1, 0.0)
                    r2 = jnp.where(i_row >= 2, r2, 0.0)
                    l1 = jnp.where(i_row <= I - 2, l1, 0.0)
                    l2 = jnp.where(i_row <= I - 3, l2, 0.0)
                total = total + ((r1 + r2) + (l1 + l2))
            out[e, k] = total
        return carry

    def chunk(c, send=True):
        flow_copy(c).wait()
        lax.fori_loop(cuts[c], cuts[c + 1], surface_terms, 0)
        if send:
            for copy in side_copies(c):
                copy.start()

    chunk(0, send=False)
    pl.semaphore_wait(barrier, NT - 1 + W - 1)
    for copy in side_copies(0):
        copy.start()
    @pl.when(w < W - 1)
    def _():
        for copy in halo_copies(0):
            copy.start()

    @pl.when(w > 0)
    def _():
        for copy in halo_copies(1):
            copy.start()

    chunk(1)
    inputs[0].wait()
    def add_total(k, total):
        layer = spacing[k]
        sp[k + 2] = layer
        return total + layer

    slab_total[...] = lax.fori_loop(0, K, add_total, jnp.zeros((I, J), f32))
    inv, vx, vy, vz, pressure = primitives_of(*[flow[e, 0] for e in range(5)])
    film_buf[0] = 2.0 / spacing[0]
    film_buf[1] = pressure * inv + 0.2 * (vx * vx + vy * vy + vz * vz)

    @pl.when(w == 0)
    def _():
        for d in range(1, W):
            film_copy(d).start()

    for d in range(1, W):
        total_copy(d).start()
    totals_in[w] = slab_total[...]

    chunk(2)

    for copy in inputs[1:]:
        copy.wait()
    cell = cells[...]
    tile = lax.shift_right_logical(cell, shift_of(I * J))
    within = jnp.bitwise_and(cell, I * J - 1)
    row_i = lax.shift_right_logical(within, shift_of(J))
    col_j = jnp.bitwise_and(within, J - 1)
    row = lax.shift_right_logical(col_j, 7) * I + row_i
    lane = jnp.bitwise_and(col_j, 127)
    zone = zones[...]
    tile_iota = lax.broadcasted_iota(jnp.int32, (NT, C), 0)
    lane_iota = lax.broadcasted_iota(jnp.int32, (NT, C), 1)
    mine = jnp.where(tile_iota == tile, 1.0, 0.0).astype(f32)
    run = mine
    step = 1
    while step < C:
        run = run + jnp.where(lane_iota >= step, pltpu.roll(run, step, 1), 0.0)
        step *= 2
    rank = jnp.sum(mine * run, axis=0, keepdims=True).astype(jnp.int32) - 1
    slot = tile * PT + rank
    V[...] = jnp.zeros(V.shape, f32)
    V[0:1, 0:C] = row.astype(f32)
    V[1:2, 0:C] = lane.astype(f32)
    V[2:3, 0:C] = zone.astype(f32)
    for n, piece in enumerate(parts3(abl[0:1, :]) + parts3(abl[1:2, :])):
        V[3 + n : 4 + n, 0:C] = piece
    payload = V[:, 0:C].astype(bf16)
    slot_iota = lax.broadcasted_iota(jnp.int32, (PT, C), 0)
    for t in range(NT):
        block = jnp.where(slot_iota + t * PT == slot, 1.0, 0.0).astype(bf16)
        PM[t * PT : (t + 1) * PT, :] = block
        got = lax.dot_general(payload, block, (((1,), (1,)), ((), ())), preferred_element_type=f32)
        send_list[t] = jnp.zeros((8, PT), f32)
        send_list[t, 0:3] = got[0:3]
        send_list[t, 3:4] = got[3:4] + got[4:5] + got[5:6]
        send_list[t, 4:5] = got[6:7] + got[7:8] + got[8:9]

    for d in range(1, NT):
        list_copy(d).start()

    for c in (3, 4, 5, 6):
        chunk(c)

    recv_list[0] = send_list[s]
    for d in range(1, NT):
        list_copy(d).wait()
    listed = jnp.concatenate([recv_list[d] for d in range(NT)], axis=1)
    count = NT * PT
    l_row = listed[0:1].astype(jnp.int32)
    l_lane = listed[1:2].astype(jnp.int32)
    row_hot = jnp.where(lax.broadcasted_iota(jnp.int32, (R, count), 0) == l_row, 1.0, 0.0)
    lane_hot = jnp.where(
        lax.broadcasted_iota(jnp.int32, (128, count), 0) == l_lane, 1.0, 0.0).astype(bf16)
    pieces = parts3(listed[3:4]) + parts3(listed[4:5]) + (listed[2:3],)
    stack = jnp.concatenate([row_hot * piece for piece in pieces], axis=0).astype(bf16)
    grid = lax.dot_general(stack, lane_hot, (((1,), (1,)), ((), ())), preferred_element_type=f32)
    first = grid[0:R] + grid[R : 2 * R] + grid[2 * R : 3 * R]
    second = grid[3 * R : 4 * R] + grid[4 * R : 5 * R] + grid[5 * R : 6 * R]
    zone_grid = grid[6 * R : 7 * R]

    @pl.when(w == 0)
    def _():
        for d in range(1, W):
            film_copy(d).wait_send()
        film_in[...] = film_buf[...]

    @pl.when(w > 0)
    def _():
        film_copy(1).wait_recv()

    film = jnp.concatenate([film_in[0, :, b * 128 : (b + 1) * 128] for b in range(JB)], axis=0)
    recov = jnp.concatenate([film_in[1, :, b * 128 : (b + 1) * 128] for b in range(JB)], axis=0)
    zone_grid = zone_grid.astype(jnp.int32)
    owned = first > 0.25
    cond = pick(zone_grid, conduct, NZ)
    surface = jnp.where(owned, first, 1.0)
    for newton_pass in range(2):
        cube = surface * surface * surface
        surface = (film * recov + cond * second + 2.4 * cube * surface) / (film + cond + 3.2 * cube)
    recess = pick(zone_grid, rate, NZ) * jnp.exp(-2.0 / surface)
    part[0] = jnp.where(owned, surface, 0.0)
    part[1] = jnp.where(owned, recess, 0.0)

    def part_copy(d):
        return pltpu.make_async_remote_copy(
            part, part_in.at[d], s_part.at[d], r_part.at[d],
            device_id=(s, lax.rem(w + d, W)), device_id_type=MESH)

    for d in range(1, W):
        part_copy(d).start()

    table = jnp.concatenate(parts3(part[0]), axis=0).astype(bf16)
    spread = jnp.dot(table, lane_hot, preferred_element_type=f32)
    spread = spread[0:R] + spread[R : 2 * R] + spread[2 * R : 3 * R]
    answer = jnp.sum(spread * row_hot, axis=0, keepdims=True)
    for d in range(NT):
        reply[d] = jnp.broadcast_to(answer[:, d * PT : (d + 1) * PT], (8, PT))

    def reply_copy(d):
        return pltpu.make_async_remote_copy(
            reply.at[d], reply_in.at[s], s_rep.at[d], r_rep.at[d],
            device_id=(lax.rem(s + NT - d, NT), w), device_id_type=MESH)

    for d in range(1, NT):
        reply_copy(d).start()
    reply_in[s] = reply[0]
    for c in range(7, chunks):
        chunk(c)

    for d in range(1, W):
        part_copy(d).wait()
    whole = part[...]
    for d in range(1, W):
        whole = whole + part_in[d]
    dense[...] = whole
    surf_temp = jnp.concatenate([dense[0, b * I : (b + 1) * I, :] for b in range(JB)], axis=1)
    surf_recess = jnp.concatenate([dense[1, b * I : (b + 1) * I, :] for b in range(JB)], axis=1)

    for d in range(1, W):
        total_copy(d).wait()
    column_total = jnp.zeros((I, J), f32)
    offset = jnp.zeros((I, J), f32)
    for n in range(W):
        column_total = column_total + totals_in[n]
        offset = offset + jnp.where(n < w, totals_in[n], 0.0)

    @pl.when(w < W - 1)
    def _():
        for copy in halo_copies(0):
            copy.wait_send()
        for copy in halo_copies(1):
            copy.wait_recv()

    @pl.when(w > 0)
    def _():
        for copy in halo_copies(1):
            copy.wait_send()
        for copy in halo_copies(0):
            copy.wait_recv()

    def put(at, values):
        flux, fields = values
        for e in range(5):
            F3[at, e] = flux[e]
        for e in range(4):
            Q[at, e] = fields[e]

    def put_halo(side, base):
        for n in range(2):
            u = [halo_u[side, e, n] for e in range(5)]
            inv, vx, vy, vz, pressure = primitives_of(*u)
            put(base + n, normal_fields(u[0], vx, vy, vz, pressure))
            sp[base + n] = halo_s[side, n]

    @pl.when(w > 0)
    def _():
        put_halo(0, 0)

    @pl.when(w < W - 1)
    def _():
        put_halo(1, K + 2)

    @pl.when(w == 0)
    def _():
        kinds = kind[...]
        slip = kinds == 1
        for n in range(2):
            u = [flow[e, n] for e in range(5)]
            inv, vx, vy, vz, pressure = primitives_of(*u)
            density = jnp.where(slip, u[0], pressure / surf_temp)
            vx = jnp.where(slip, vx, -vx)
            vy = jnp.where(slip, vy, -vy)
            vz = jnp.where(kinds == 2, 2.0 * surf_recess - vz, -vz)
            put(1 - n, normal_fields(density, vx, vy, vz, pressure))
        sp[1] = spacing[1]
        sp[0] = spacing[0]

    @pl.when(w == W - 1)
    def _():
        one = jnp.full((I, J), 1.0, f32)
        zero = jnp.zeros((I, J), f32)
        for n in range(2):
            put(K + 2 + n, normal_fields(one, 0.5 * one, zero, zero, one))
        sp[K + 2] = spacing[K - 2]
        sp[K + 3] = spacing[K - 1]

    inv_total = 1.0 / column_total
    stretch = (1.0 + surf_recess * inv_total) * (1.0 / 12.0)

    def normal_terms(k, run):
        here = sp[k + 2]
        metric = stretch * (
            3.0 * (sp[k + 1] + sp[k + 3]) + 7.0 * here - 0.5 * (sp[k] + sp[k + 4]))
        inv_metric = 1.0 / metric
        inv_square = inv_metric * inv_metric
        normalized = (run + 0.5 * here) * inv_total
        shift_out[k] = surf_recess * (normalized - 1.0)
        damp = (time_step * sponge_rate) * normalized * normalized
        for e in range(5):
            diff = 8.0 * (F3[k + 3, e] - F3[k + 1, e]) - (F3[k + 4, e] - F3[k, e])
            total = out[e, k] - inv_metric * diff - damp * (flow[e, k] - far_values[e])
            if e:
                lap = (16.0 * (Q[k + 3, e - 1] + Q[k + 1, e - 1])
                       - (Q[k + 4, e - 1] + Q[k, e - 1]) - 30.0 * Q[k + 2, e - 1])
                total = total + inv_square * lap
            out[e, k] = total
        return run + here

    lax.fori_loop(0, K, normal_terms, offset)
    shift_copy = pltpu.make_async_copy(shift_out, shift_hbm, s_out.at[0])
    shift_copy.start()
    out_copy = pltpu.make_async_copy(out, out_hbm, s_out.at[2])
    out_copy.start()

    for d in range(1, NT):
        reply_copy(d).wait()
    answer = jnp.concatenate([reply_in[t, 0:1] for t in range(NT)], axis=1)
    V[...] = jnp.zeros(V.shape, f32)
    for n, piece in enumerate(parts3(answer)):
        V[n : n + 1, 0:count] = piece
    back = jnp.dot(V[:, 0:count].astype(bf16), PM[...], preferred_element_type=f32)
    col_surface = back[0:1] + back[1:2] + back[2:3]
    col_diffuse = pick(zone, diffuse, NZ)
    depth = abl.shape[0]
    depth_row = lax.broadcasted_iota(jnp.int32, (depth, C), 0)
    profile = jnp.where(depth_row == 0, col_surface, abl[...])
    for heat_pass in range(2):
        below = pltpu.roll(profile, 1, 0)
        above = jnp.where(depth_row == depth - 1, below, pltpu.roll(profile, depth - 1, 0))
        gain = col_diffuse * (above - 2.0 * profile + below)
        profile = jnp.where(depth_row == 0, profile, profile + gain)
    abl_out[...] = profile
    abl_copy = pltpu.make_async_copy(abl_out, abl_out_hbm, s_out.at[1])
    abl_copy.start()

    for c in range(chunks):
        for copy in side_copies(c):
            copy.wait()
    shift_copy.wait()
    abl_copy.wait()
    out_copy.wait()


def hand_out(
    state_in, shift_in, abl_in, RL_in, RR_in,
    state_hbm, shift_hbm, abl_hbm,
    state, shift, abl, RL, RR, s_in, s_out,
):
    K, I = state.shape[1], state.shape[2]
    size = K // HAND

    def loads(c):
        ks = pl.ds(c * size, size)
        return (
            pltpu.make_async_copy(RL_in.at[ks], RL.at[ks], s_in.at[0, c]),
            pltpu.make_async_copy(RR_in.at[ks], RR.at[ks], s_in.at[1, c]),
            pltpu.make_async_copy(state_in.at[:, ks], state.at[:, ks], s_in.at[2, c]),
        )

    def store(c):
        ks = pl.ds(c * size, size)
        return pltpu.make_async_copy(state.at[:, ks], state_hbm.at[:, ks], s_out.at[c])

    def add_sides(k, carry):
        for e in range(5):
            state[e, k, 0:2] = state[e, k, 0:2] + RL[k, e]
            state[e, k, I - 2 : I] = state[e, k, I - 2 : I] + RR[k, e]
        return carry

    rest = ((shift_in, shift, shift_hbm), (abl_in, abl, abl_hbm))
    rest_in = [pltpu.make_async_copy(a, b, s_in.at[n, HAND]) for n, (a, b, _) in enumerate(rest)]
    rest_out = [pltpu.make_async_copy(b, c, s_out.at[HAND + n]) for n, (_, b, c) in enumerate(rest)]
    for c in range(HAND):
        for copy in loads(c):
            copy.start()
    for copy in rest_in:
        copy.start()
    for c in range(HAND):
        for copy in loads(c):
            copy.wait()
        lax.fori_loop(c * size, (c + 1) * size, add_sides, 0)
        store(c).start()
    for copy, later in zip(rest_in, rest_out):
        copy.wait()
        later.start()
    for c in range(HAND):
        store(c).wait()
    for copy in rest_out:
        copy.wait()


def shards(flow_state, spacing, bc_kind, cell_of, zone_id, abl_temp, conduct, diffuse, rate):
    NT = lax.axis_size("surf")
    W = lax.axis_size("wall")
    K, I, J = spacing.shape
    C = cell_of.shape[0]
    PT = -(-(C // NT) // 128) * 128
    R = I * J // 128
    count = NT * PT
    dims = (K, I, J, NT, W, C, PT, conduct.shape[0])
    dma = pltpu.SemaphoreType.DMA
    chunks = len(bounds_of(K)) - 1
    scratch = [
        pltpu.VMEM(flow_state.shape, f32),
        pltpu.VMEM(spacing.shape, f32),
        pltpu.VMEM(abl_temp.shape, f32),
        dma((3,)),
        pltpu.VMEM(flow_state.shape, f32),
        pltpu.VMEM(spacing.shape, f32),
        pltpu.VMEM(bc_kind.shape, jnp.int32),
        pltpu.VMEM((1, C), jnp.int32),
        pltpu.VMEM((1, C), jnp.int32),
        pltpu.VMEM(abl_temp.shape, f32),
        pltpu.SMEM(conduct.shape, f32),
        pltpu.SMEM(conduct.shape, f32),
        pltpu.SMEM(conduct.shape, f32),
        dma((chunks,)), dma((8,)),
        pltpu.VMEM((K + 4, 5, I, J), f32),
        pltpu.VMEM((K + 4, 4, I, J), f32),
        pltpu.VMEM((K, 5, 2, J), f32),
        pltpu.VMEM((K, 5, 2, J), f32),
        pltpu.VMEM((count, C), bf16),
        pltpu.VMEM((16, max(C, count)), f32),
        pltpu.VMEM((NT, 8, PT), f32),
        pltpu.VMEM((NT, 8, PT), f32),
        pltpu.VMEM((NT, 8, PT), f32),
        pltpu.VMEM((NT, 8, PT), f32),
        pltpu.VMEM((I, J), f32),
        pltpu.VMEM((W, I, J), f32),
        pltpu.VMEM((2, I, J), f32),
        pltpu.VMEM((2, I, J), f32),
        pltpu.VMEM((2, R, 128), f32),
        pltpu.VMEM((W, 2, R, 128), f32),
        pltpu.VMEM((2, 5, 2, I, J), f32),
        pltpu.VMEM((2, 2, I, J), f32),
        pltpu.VMEM((K + 4, I, J), f32),
        pltpu.VMEM((2, R, 128), f32),
        dma((NT,)), dma((NT,)), dma((NT,)), dma((NT,)),
        dma((W,)), dma((W,)), dma((W,)), dma,
        dma((W,)), dma((W,)),
        dma((2,)), dma((2,)), dma((2,)), dma((2,)),
        dma((2, chunks)), dma((2, chunks)),
    ]
    hbm = pl.BlockSpec(memory_space=pltpu.HBM)
    results = pl.pallas_call(
        functools.partial(kernel, dims),
        out_shape=(
            jax.ShapeDtypeStruct(flow_state.shape, f32),
            jax.ShapeDtypeStruct(spacing.shape, f32),
            jax.ShapeDtypeStruct(abl_temp.shape, f32),
            jax.ShapeDtypeStruct((K, 5, 2, J), f32),
            jax.ShapeDtypeStruct((K, 5, 2, J), f32),
        ),
        in_specs=[hbm] * 9,
        out_specs=(hbm,) * 5,
        scratch_shapes=scratch,
        compiler_params=pltpu.CompilerParams(
            collective_id=0, has_side_effects=True, vmem_limit_bytes=VMEM_BYTES),
    )(flow_state, spacing, bc_kind, cell_of.reshape(1, C), zone_id.reshape(1, C), abl_temp,
      conduct, diffuse, rate)
    return pl.pallas_call(
        hand_out,
        out_shape=[jax.ShapeDtypeStruct(r.shape, f32) for r in results[:3]],
        in_specs=[hbm] * 5,
        out_specs=[hbm] * 3,
        scratch_shapes=[pltpu.VMEM(r.shape, f32) for r in results] + [dma((3, HAND + 1)), dma((HAND + 2,))],
        compiler_params=pltpu.CompilerParams(vmem_limit_bytes=VMEM_BYTES),
    )(*results)


def solution(mesh):
    in_specs = (
        P(None, "wall", "surf", None),
        P("wall", "surf", None),
        P("surf", None),
        P(("surf", "wall")),
        P(("surf", "wall")),
        P(None, ("surf", "wall")),
        P(),
        P(),
        P(),
    )
    out_specs = (P(None, "wall", "surf", None), P("wall", "surf", None), P(None, ("surf", "wall")))
    return jax.shard_map(shards, mesh=mesh, in_specs=in_specs, out_specs=out_specs, check_vma=False)
```

```python
import functools

import jax
import jax.numpy as jnp
from jax import lax
from jax.experimental import pallas as pl
from jax.experimental.pallas import tpu as pltpu
from jax.sharding import PartitionSpec as P

f32 = jnp.float32
bf16 = jnp.bfloat16
MESH = pl.DeviceIdType.MESH

time_step = 0.15
viscosity = 0.05
conduction = 0.07
sponge_rate = 0.5
far_values = (1.0, 0.5, 0.0, 0.0, 2.625)
SCALE = time_step / 12.0
CHUNK = 4
HAND = 4
VMEM_BYTES = 26 * 1024 * 1024


def bounds_of(K):
    return (0, 2) + tuple(range(4, K + 1, CHUNK))


def parts3(x):
    a = x.astype(bf16).astype(f32)
    b = (x - a).astype(bf16).astype(f32)
    c = (x - a - b).astype(bf16).astype(f32)
    return a, b, c


def shift_of(n):
    assert n & (n - 1) == 0
    return n.bit_length() - 1


def pick(index, table_ref, count):
    out = jnp.zeros(index.shape, f32)
    for z in range(count):
        out = jnp.where(index == z, table_ref[z], out)
    return out


def normal_fields(density, vx, vy, vz, pressure):
    energy = 2.5 * pressure + 0.5 * density * (vx * vx + vy * vy + vz * vz)
    svz = SCALE * vz
    rho_w = density * svz
    flux = (
        rho_w,
        rho_w * vx,
        rho_w * vy,
        rho_w * vz + SCALE * pressure,
        (energy + pressure) * svz,
    )
    cv = SCALE * viscosity
    return flux, (cv * vx, cv * vy, cv * vz, (SCALE * conduction) * (pressure / density))


def primitives_of(u0, u1, u2, u3, u4):
    inv = 1.0 / u0
    vx, vy, vz = u1 * inv, u2 * inv, u3 * inv
    pressure = 0.4 * (u4 - 0.5 * (u1 * vx + u2 * vy + u3 * vz))
    return inv, vx, vy, vz, pressure


def kernel(
    dims,
    flow_hbm, spacing_hbm, kind_hbm, cells_hbm, zones_hbm, abl_hbm, conduct_hbm, diffuse_hbm, rate_hbm,
    out, shift_out, abl_out, RL, RR,
    flow, spacing, kind, cells, zones, abl, conduct, diffuse, rate, s_flow, s_in,
    F3, Q, XR, XL, PM, V, send_list, recv_list, reply, reply_in,
    slab_total, totals_in, film_buf, film_in, part, part_in,
    halo_u, halo_s, sp, dense,
    s_list, r_list, s_rep, r_rep, s_tot, r_tot, s_film, r_film, s_part, r_part,
    s_hu, r_hu, s_hs, r_hs, s_x, r_x,
):
    K, I, J, NT, W, C, PT, NZ = dims
    R = I * J // 128
    JB = J // 128
    s = lax.axis_index("surf")
    w = lax.axis_index("wall")

    cuts = bounds_of(K)
    chunks = len(cuts) - 1

    def flow_copy(c):
        ks = pl.ds(cuts[c], cuts[c + 1] - cuts[c])
        return pltpu.make_async_copy(flow_hbm.at[:, ks], flow.at[:, ks], s_flow.at[c])

    pairs = ((spacing_hbm, spacing), (cells_hbm, cells), (zones_hbm, zones), (abl_hbm, abl),
             (kind_hbm, kind), (conduct_hbm, conduct), (diffuse_hbm, diffuse), (rate_hbm, rate))
    inputs = [pltpu.make_async_copy(a, b, s_in.at[n]) for n, (a, b) in enumerate(pairs)]
    flow_copy(0).start()
    for copy in inputs:
        copy.start()
    for c in range(1, chunks):
        flow_copy(c).start()
    barrier = pltpu.get_barrier_semaphore()
    for d in range(1, NT):
        pl.semaphore_signal(barrier, inc=1, device_id=(lax.rem(s + d, NT), w), device_id_type=MESH)
    for d in range(1, W):
        pl.semaphore_signal(barrier, inc=1, device_id=(s, lax.rem(w + d, W)), device_id_type=MESH)

    def list_copy(d):
        t = lax.rem(s + d, NT)
        return pltpu.make_async_remote_copy(
            send_list.at[t], recv_list.at[d], s_list.at[d], r_list.at[d],
            device_id=(t, w), device_id_type=MESH)

    def total_copy(d):
        return pltpu.make_async_remote_copy(
            slab_total, totals_in.at[w], s_tot.at[d], r_tot.at[d],
            device_id=(s, lax.rem(w + d, W)), device_id_type=MESH)

    def film_copy(d):
        return pltpu.make_async_remote_copy(
            film_buf, film_in, s_film.at[d], r_film,
            device_id=(s, lax.rem(w + d, W)), device_id_type=MESH)

    def halo_copies(side):
        near, target = (K - 2, lax.rem(w + 1, W)) if side == 0 else (0, lax.rem(w + W - 1, W))
        return (
            pltpu.make_async_remote_copy(
                flow_hbm.at[:, near : near + 2], halo_u.at[side], s_hu.at[side], r_hu.at[side],
                device_id=(s, target), device_id_type=MESH),
            pltpu.make_async_remote_copy(
                spacing_hbm.at[near : near + 2], halo_s.at[side], s_hs.at[side], r_hs.at[side],
                device_id=(s, target), device_id_type=MESH),
        )

    def side_copies(c):
        ks = pl.ds(cuts[c], cuts[c + 1] - cuts[c])
        return (
            pltpu.make_async_remote_copy(
                XR.at[ks], RL.at[ks], s_x.at[0, c], r_x.at[0, c],
                device_id=(lax.rem(s + 1, NT), w), device_id_type=MESH),
            pltpu.make_async_remote_copy(
                XL.at[ks], RR.at[ks], s_x.at[1, c], r_x.at[1, c],
                device_id=(lax.rem(s + NT - 1, NT), w), device_id_type=MESH),
        )

    i_row = lax.broadcasted_iota(jnp.int32, (I, J), 0)

    def surface_terms(k, carry):
        u = [flow[e, k] for e in range(5)]
        inv, vx, vy, vz, pressure = primitives_of(*u)
        enthalpy = u[4] + pressure
        sx, sy, sz, sp_ = SCALE * vx, SCALE * vy, SCALE * vz, SCALE * pressure
        m12, m13, m23 = u[1] * sy, u[1] * sz, u[2] * sz
        q = (viscosity * sx, viscosity * sy, viscosity * sz,
             (conduction * inv) * sp_)
        f1 = (SCALE * u[1], u[1] * sx + sp_, m12, m13, enthalpy * sx)
        f2 = (SCALE * u[2], m12, u[2] * sy + sp_, m23, enthalpy * sy)
        f3 = (SCALE * u[3], m13, m23, u[3] * sz + sp_, enthalpy * sz)
        for e in range(5):
            F3[k + 2, e] = f3[e]
        for e in range(4):
            Q[k + 2, e] = q[e]
        for e in range(5):
            total = u[e]
            if e:
                qe = q[e - 1]
                total = total - 60.0 * qe
                q8 = 8.0 * qe
            for axis, size, flux in ((0, I, f1[e]), (1, J, f2[e])):
                if e:
                    up2 = flux - qe
                    down2 = -flux - qe
                    up1 = q8 - 8.0 * up2
                    down1 = q8 - 8.0 * down2
                else:
                    up2 = flux
                    down2 = -flux
                    up1 = -8.0 * flux
                    down1 = 8.0 * flux
                r1 = pltpu.roll(down1, 1, axis)
                r2 = pltpu.roll(down2, 2, axis)
                l1 = pltpu.roll(up1, size - 1, axis)
                l2 = pltpu.roll(up2, size - 2, axis)
                if axis == 0:
                    to_right = r2 + jnp.where(i_row == 0, r1, 0.0)
                    to_left = up2 + jnp.where(i_row == 1, pltpu.roll(up1, 1, 0), 0.0)
                    XR[k, e] = to_right[0:2]
                    XL[k, e] = to_left[0:2]
                    r1 = jnp.where(i_row >= 1, r1, 0.0)
                    r2 = jnp.where(i_row >= 2, r2, 0.0)
                    l1 = jnp.where(i_row <= I - 2, l1, 0.0)
                    l2 = jnp.where(i_row <= I - 3, l2, 0.0)
                total = total + ((r1 + r2) + (l1 + l2))
            out[e, k] = total
        return carry

    def chunk(c, send=True):
        flow_copy(c).wait()
        lax.fori_loop(cuts[c], cuts[c + 1], surface_terms, 0)
        if send:
            for copy in side_copies(c):
                copy.start()

    chunk(0, send=False)
    pl.semaphore_wait(barrier, NT - 1 + W - 1)
    for copy in side_copies(0):
        copy.start()
    @pl.when(w < W - 1)
    def _():
        for copy in halo_copies(0):
            copy.start()

    @pl.when(w > 0)
    def _():
        for copy in halo_copies(1):
            copy.start()

    chunk(1)
    inputs[0].wait()
    def add_total(k, total):
        layer = spacing[k]
        sp[k + 2] = layer
        return total + layer

    slab_total[...] = lax.fori_loop(0, K, add_total, jnp.zeros((I, J), f32))
    inv, vx, vy, vz, pressure = primitives_of(*[flow[e, 0] for e in range(5)])
    film_buf[0] = 2.0 / spacing[0]
    film_buf[1] = pressure * inv + 0.2 * (vx * vx + vy * vy + vz * vz)

    @pl.when(w == 0)
    def _():
        for d in range(1, W):
            film_copy(d).start()

    for d in range(1, W):
        total_copy(d).start()
    totals_in[w] = slab_total[...]

    chunk(2)

    for copy in inputs[1:]:
        copy.wait()
    cell = cells[...]
    tile = lax.shift_right_logical(cell, shift_of(I * J))
    within = jnp.bitwise_and(cell, I * J - 1)
    row_i = lax.shift_right_logical(within, shift_of(J))
    col_j = jnp.bitwise_and(within, J - 1)
    row = lax.shift_right_logical(col_j, 7) * I + row_i
    lane = jnp.bitwise_and(col_j, 127)
    zone = zones[...]
    tile_iota = lax.broadcasted_iota(jnp.int32, (NT, C), 0)
    lane_iota = lax.broadcasted_iota(jnp.int32, (NT, C), 1)
    mine = jnp.where(tile_iota == tile, 1.0, 0.0).astype(f32)
    run = mine
    step = 1
    while step < C:
        run = run + jnp.where(lane_iota >= step, pltpu.roll(run, step, 1), 0.0)
        step *= 2
    rank = jnp.sum(mine * run, axis=0, keepdims=True).astype(jnp.int32) - 1
    slot = tile * PT + rank
    V[...] = jnp.zeros(V.shape, f32)
    V[0:1, 0:C] = row.astype(f32)
    V[1:2, 0:C] = lane.astype(f32)
    V[2:3, 0:C] = zone.astype(f32)
    for n, piece in enumerate(parts3(abl[0:1, :]) + parts3(abl[1:2, :])):
        V[3 + n : 4 + n, 0:C] = piece
    payload = V[:, 0:C].astype(bf16)
    slot_iota = lax.broadcasted_iota(jnp.int32, (PT, C), 0)
    for t in range(NT):
        block = jnp.where(slot_iota + t * PT == slot, 1.0, 0.0).astype(bf16)
        PM[t * PT : (t + 1) * PT, :] = block
        got = lax.dot_general(payload, block, (((1,), (1,)), ((), ())), preferred_element_type=f32)
        send_list[t] = jnp.zeros((8, PT), f32)
        send_list[t, 0:3] = got[0:3]
        send_list[t, 3:4] = got[3:4] + got[4:5] + got[5:6]
        send_list[t, 4:5] = got[6:7] + got[7:8] + got[8:9]

    for d in range(1, NT):
        list_copy(d).start()

    for c in (3, 4, 5, 6):
        chunk(c)

    recv_list[0] = send_list[s]
    for d in range(1, NT):
        list_copy(d).wait()
    listed = jnp.concatenate([recv_list[d] for d in range(NT)], axis=1)
    count = NT * PT
    l_row = listed[0:1].astype(jnp.int32)
    l_lane = listed[1:2].astype(jnp.int32)
    row_hot = jnp.where(lax.broadcasted_iota(jnp.int32, (R, count), 0) == l_row, 1.0, 0.0)
    lane_hot = jnp.where(
        lax.broadcasted_iota(jnp.int32, (128, count), 0) == l_lane, 1.0, 0.0).astype(bf16)
    pieces = parts3(listed[3:4]) + parts3(listed[4:5]) + (listed[2:3],)
    stack = jnp.concatenate([row_hot * piece for piece in pieces], axis=0).astype(bf16)
    grid = lax.dot_general(stack, lane_hot, (((1,), (1,)), ((), ())), preferred_element_type=f32)
    first = grid[0:R] + grid[R : 2 * R] + grid[2 * R : 3 * R]
    second = grid[3 * R : 4 * R] + grid[4 * R : 5 * R] + grid[5 * R : 6 * R]
    zone_grid = grid[6 * R : 7 * R]

    @pl.when(w == 0)
    def _():
        for d in range(1, W):
            film_copy(d).wait_send()
        film_in[...] = film_buf[...]

    @pl.when(w > 0)
    def _():
        film_copy(1).wait_recv()

    film = jnp.concatenate([film_in[0, :, b * 128 : (b + 1) * 128] for b in range(JB)], axis=0)
    recov = jnp.concatenate([film_in[1, :, b * 128 : (b + 1) * 128] for b in range(JB)], axis=0)
    zone_grid = zone_grid.astype(jnp.int32)
    owned = first > 0.25
    cond = pick(zone_grid, conduct, NZ)
    surface = jnp.where(owned, first, 1.0)
    for newton_pass in range(2):
        cube = surface * surface * surface
        surface = (film * recov + cond * second + 2.4 * cube * surface) / (film + cond + 3.2 * cube)
    recess = pick(zone_grid, rate, NZ) * jnp.exp(-2.0 / surface)
    part[0] = jnp.where(owned, surface, 0.0)
    part[1] = jnp.where(owned, recess, 0.0)

    def part_copy(d):
        return pltpu.make_async_remote_copy(
            part, part_in.at[d], s_part.at[d], r_part.at[d],
            device_id=(s, lax.rem(w + d, W)), device_id_type=MESH)

    for d in range(1, W):
        part_copy(d).start()

    table = jnp.concatenate(parts3(part[0]), axis=0).astype(bf16)
    spread = jnp.dot(table, lane_hot, preferred_element_type=f32)
    spread = spread[0:R] + spread[R : 2 * R] + spread[2 * R : 3 * R]
    answer = jnp.sum(spread * row_hot, axis=0, keepdims=True)
    for d in range(NT):
        reply[d] = jnp.broadcast_to(answer[:, d * PT : (d + 1) * PT], (8, PT))

    def reply_copy(d):
        return pltpu.make_async_remote_copy(
            reply.at[d], reply_in.at[s], s_rep.at[d], r_rep.at[d],
            device_id=(lax.rem(s + NT - d, NT), w), device_id_type=MESH)

    for d in range(1, NT):
        reply_copy(d).start()
    reply_in[s] = reply[0]
    for c in range(7, chunks):
        chunk(c)

    for d in range(1, W):
        part_copy(d).wait()
    whole = part[...]
    for d in range(1, W):
        whole = whole + part_in[d]
    dense[...] = whole
    surf_temp = jnp.concatenate([dense[0, b * I : (b + 1) * I, :] for b in range(JB)], axis=1)
    surf_recess = jnp.concatenate([dense[1, b * I : (b + 1) * I, :] for b in range(JB)], axis=1)

    for d in range(1, W):
        total_copy(d).wait()
    column_total = jnp.zeros((I, J), f32)
    offset = jnp.zeros((I, J), f32)
    for n in range(W):
        column_total = column_total + totals_in[n]
        offset = offset + jnp.where(n < w, totals_in[n], 0.0)

    @pl.when(w < W - 1)
    def _():
        for copy in halo_copies(0):
            copy.wait_send()
        for copy in halo_copies(1):
            copy.wait_recv()

    @pl.when(w > 0)
    def _():
        for copy in halo_copies(1):
            copy.wait_send()
        for copy in halo_copies(0):
            copy.wait_recv()

    def put(at, values):
        flux, fields = values
        for e in range(5):
            F3[at, e] = flux[e]
        for e in range(4):
            Q[at, e] = fields[e]

    def put_halo(side, base):
        for n in range(2):
            u = [halo_u[side, e, n] for e in range(5)]
            inv, vx, vy, vz, pressure = primitives_of(*u)
            put(base + n, normal_fields(u[0], vx, vy, vz, pressure))
            sp[base + n] = halo_s[side, n]

    @pl.when(w > 0)
    def _():
        put_halo(0, 0)

    @pl.when(w < W - 1)
    def _():
        put_halo(1, K + 2)

    @pl.when(w == 0)
    def _():
        kinds = kind[...]
        slip = kinds == 1
        for n in range(2):
            u = [flow[e, n] for e in range(5)]
            inv, vx, vy, vz, pressure = primitives_of(*u)
            density = jnp.where(slip, u[0], pressure / surf_temp)
            vx = jnp.where(slip, vx, -vx)
            vy = jnp.where(slip, vy, -vy)
            vz = jnp.where(kinds == 2, 2.0 * surf_recess - vz, -vz)
            put(1 - n, normal_fields(density, vx, vy, vz, pressure))
        sp[1] = spacing[1]
        sp[0] = spacing[0]

    @pl.when(w == W - 1)
    def _():
        one = jnp.full((I, J), 1.0, f32)
        zero = jnp.zeros((I, J), f32)
        for n in range(2):
            put(K + 2 + n, normal_fields(one, 0.5 * one, zero, zero, one))
        sp[K + 2] = spacing[K - 2]
        sp[K + 3] = spacing[K - 1]

    inv_total = 1.0 / column_total
    stretch = (1.0 + surf_recess * inv_total) * (1.0 / 12.0)

    def normal_terms(k, run):
        here = sp[k + 2]
        metric = stretch * (
            3.0 * (sp[k + 1] + sp[k + 3]) + 7.0 * here - 0.5 * (sp[k] + sp[k + 4]))
        inv_metric = 1.0 / metric
        inv_square = inv_metric * inv_metric
        normalized = (run + 0.5 * here) * inv_total
        shift_out[k] = surf_recess * (normalized - 1.0)
        damp = (time_step * sponge_rate) * normalized * normalized
        for e in range(5):
            diff = 8.0 * (F3[k + 3, e] - F3[k + 1, e]) - (F3[k + 4, e] - F3[k, e])
            total = out[e, k] - inv_metric * diff - damp * (flow[e, k] - far_values[e])
            if e:
                lap = (16.0 * (Q[k + 3, e - 1] + Q[k + 1, e - 1])
                       - (Q[k + 4, e - 1] + Q[k, e - 1]) - 30.0 * Q[k + 2, e - 1])
                total = total + inv_square * lap
            out[e, k] = total
        return run + here

    lax.fori_loop(0, K, normal_terms, offset)

    for d in range(1, NT):
        reply_copy(d).wait()
    answer = jnp.concatenate([reply_in[t, 0:1] for t in range(NT)], axis=1)
    V[...] = jnp.zeros(V.shape, f32)
    for n, piece in enumerate(parts3(answer)):
        V[n : n + 1, 0:count] = piece
    back = jnp.dot(V[:, 0:count].astype(bf16), PM[...], preferred_element_type=f32)
    col_surface = back[0:1] + back[1:2] + back[2:3]
    col_diffuse = pick(zone, diffuse, NZ)
    depth = abl.shape[0]
    depth_row = lax.broadcasted_iota(jnp.int32, (depth, C), 0)
    profile = jnp.where(depth_row == 0, col_surface, abl[...])
    for heat_pass in range(2):
        below = pltpu.roll(profile, 1, 0)
        above = jnp.where(depth_row == depth - 1, below, pltpu.roll(profile, depth - 1, 0))
        gain = col_diffuse * (above - 2.0 * profile + below)
        profile = jnp.where(depth_row == 0, profile, profile + gain)
    abl_out[...] = profile

    for c in range(chunks):
        for copy in side_copies(c):
            copy.wait()


def hand_out(state_in, shift, abl, RL, RR, state_hbm, shift_hbm, abl_hbm, state, s_out):
    K, I, J = state.shape[1:]
    size = K // HAND

    def store(c):
        ks = pl.ds(c * size, size)
        return pltpu.make_async_copy(state.at[:, ks], state_hbm.at[:, ks], s_out.at[c])

    def add_sides(k, carry):
        for e in range(5):
            middle = jnp.zeros((I - 4, J), f32)
            state[e, k] = state_in[e, k] + jnp.concatenate([RL[k, e], middle, RR[k, e]], axis=0)
        return carry

    rest = (pltpu.make_async_copy(shift, shift_hbm, s_out.at[HAND]),
            pltpu.make_async_copy(abl, abl_hbm, s_out.at[HAND + 1]))
    for copy in rest:
        copy.start()
    for c in range(HAND):
        lax.fori_loop(c * size, (c + 1) * size, add_sides, 0)
        store(c).start()
    for c in range(HAND):
        store(c).wait()
    for copy in rest:
        copy.wait()


def shards(flow_state, spacing, bc_kind, cell_of, zone_id, abl_temp, conduct, diffuse, rate):
    NT = lax.axis_size("surf")
    W = lax.axis_size("wall")
    K, I, J = spacing.shape
    C = cell_of.shape[0]
    PT = -(-(C // NT) // 128) * 128
    R = I * J // 128
    count = NT * PT
    dims = (K, I, J, NT, W, C, PT, conduct.shape[0])
    dma = pltpu.SemaphoreType.DMA
    chunks = len(bounds_of(K)) - 1
    scratch = [
        pltpu.VMEM(flow_state.shape, f32),
        pltpu.VMEM(spacing.shape, f32),
        pltpu.VMEM(bc_kind.shape, jnp.int32),
        pltpu.VMEM((1, C), jnp.int32),
        pltpu.VMEM((1, C), jnp.int32),
        pltpu.VMEM(abl_temp.shape, f32),
        pltpu.SMEM(conduct.shape, f32),
        pltpu.SMEM(conduct.shape, f32),
        pltpu.SMEM(conduct.shape, f32),
        dma((chunks,)), dma((8,)),
        pltpu.VMEM((K + 4, 5, I, J), f32),
        pltpu.VMEM((K + 4, 4, I, J), f32),
        pltpu.VMEM((K, 5, 2, J), f32),
        pltpu.VMEM((K, 5, 2, J), f32),
        pltpu.VMEM((count, C), bf16),
        pltpu.VMEM((16, max(C, count)), f32),
        pltpu.VMEM((NT, 8, PT), f32),
        pltpu.VMEM((NT, 8, PT), f32),
        pltpu.VMEM((NT, 8, PT), f32),
        pltpu.VMEM((NT, 8, PT), f32),
        pltpu.VMEM((I, J), f32),
        pltpu.VMEM((W, I, J), f32),
        pltpu.VMEM((2, I, J), f32),
        pltpu.VMEM((2, I, J), f32),
        pltpu.VMEM((2, R, 128), f32),
        pltpu.VMEM((W, 2, R, 128), f32),
        pltpu.VMEM((2, 5, 2, I, J), f32),
        pltpu.VMEM((2, 2, I, J), f32),
        pltpu.VMEM((K + 4, I, J), f32),
        pltpu.VMEM((2, R, 128), f32),
        dma((NT,)), dma((NT,)), dma((NT,)), dma((NT,)),
        dma((W,)), dma((W,)), dma((W,)), dma,
        dma((W,)), dma((W,)),
        dma((2,)), dma((2,)), dma((2,)), dma((2,)),
        dma((2, chunks)), dma((2, chunks)),
    ]
    hbm = pl.BlockSpec(memory_space=pltpu.HBM)
    vmem = pl.BlockSpec(memory_space=pltpu.VMEM)
    held = [pltpu.with_memory_space_constraint(x, pltpu.HBM) for x in (
        flow_state, spacing, bc_kind, cell_of.reshape(1, C), zone_id.reshape(1, C), abl_temp,
        conduct, diffuse, rate)]
    results = pl.pallas_call(
        functools.partial(kernel, dims),
        out_shape=(
            jax.ShapeDtypeStruct(flow_state.shape, f32),
            jax.ShapeDtypeStruct(spacing.shape, f32),
            jax.ShapeDtypeStruct(abl_temp.shape, f32),
            jax.ShapeDtypeStruct((K, 5, 2, J), f32),
            jax.ShapeDtypeStruct((K, 5, 2, J), f32),
        ),
        in_specs=[hbm] * 9,
        out_specs=(vmem,) * 5,
        scratch_shapes=scratch,
        compiler_params=pltpu.CompilerParams(
            collective_id=0, has_side_effects=True, vmem_limit_bytes=VMEM_BYTES),
    )(*held)
    return pl.pallas_call(
        hand_out,
        out_shape=[jax.ShapeDtypeStruct(r.shape, f32) for r in results[:3]],
        in_specs=[vmem] * 5,
        out_specs=[hbm] * 3,
        scratch_shapes=[pltpu.VMEM(flow_state.shape, f32), dma((HAND + 2,))],
        compiler_params=pltpu.CompilerParams(vmem_limit_bytes=VMEM_BYTES),
    )(*results)


def solution(mesh):
    in_specs = (
        P(None, "wall", "surf", None),
        P("wall", "surf", None),
        P("surf", None),
        P(("surf", "wall")),
        P(("surf", "wall")),
        P(None, ("surf", "wall")),
        P(),
        P(),
        P(),
    )
    out_specs = (P(None, "wall", "surf", None), P("wall", "surf", None), P(None, ("surf", "wall")))
    return jax.shard_map(shards, mesh=mesh, in_specs=in_specs, out_specs=out_specs, check_vma=False)
```

```python
import functools

import jax
import jax.numpy as jnp
from jax import lax
from jax.experimental import pallas as pl
from jax.experimental.pallas import tpu as pltpu
from jax.sharding import PartitionSpec as P

f32 = jnp.float32
bf16 = jnp.bfloat16
MESH = pl.DeviceIdType.MESH

time_step = 0.15
viscosity = 0.05
conduction = 0.07
sponge_rate = 0.5
far_values = (1.0, 0.5, 0.0, 0.0, 2.625)
SCALE = time_step / 12.0
CHUNK = 4
HAND = 4
VMEM_BYTES = 26 * 1024 * 1024


def bounds_of(K):
    return (0, 2) + tuple(range(4, K + 1, CHUNK))


def parts3(x):
    a = x.astype(bf16).astype(f32)
    b = (x - a).astype(bf16).astype(f32)
    c = (x - a - b).astype(bf16).astype(f32)
    return a, b, c


def shift_of(n):
    assert n & (n - 1) == 0
    return n.bit_length() - 1


def pick(index, table_ref, count):
    out = jnp.zeros(index.shape, f32)
    for z in range(count):
        out = jnp.where(index == z, table_ref[z], out)
    return out


def normal_fields(density, vx, vy, vz, pressure):
    energy = 2.5 * pressure + 0.5 * density * (vx * vx + vy * vy + vz * vz)
    svz = SCALE * vz
    rho_w = density * svz
    flux = (
        rho_w,
        rho_w * vx,
        rho_w * vy,
        rho_w * vz + SCALE * pressure,
        (energy + pressure) * svz,
    )
    cv = SCALE * viscosity
    return flux, (cv * vx, cv * vy, cv * vz, (SCALE * conduction) * (pressure / density))


def primitives_of(u0, u1, u2, u3, u4):
    inv = 1.0 / u0
    vx, vy, vz = u1 * inv, u2 * inv, u3 * inv
    pressure = 0.4 * (u4 - 0.5 * (u1 * vx + u2 * vy + u3 * vz))
    return inv, vx, vy, vz, pressure


def kernel(
    dims,
    flow_hbm, spacing_hbm, kind_hbm, cells_hbm, zones_hbm, abl_hbm, conduct_hbm, diffuse_hbm, rate_hbm,
    out, shift_out, abl_out, RL, RR,
    flow, spacing, kind, cells, zones, abl, conduct, diffuse, rate, s_flow, s_in,
    F3, Q, XR, XL, PM, V, send_list, recv_list, reply, reply_in,
    slab_total, totals_in, film_buf, film_in, part, part_in,
    halo_u, halo_s, sp, dense,
    s_list, r_list, s_rep, r_rep, s_tot, r_tot, s_film, r_film, s_part, r_part,
    s_hu, r_hu, s_hs, r_hs, s_x, r_x,
):
    K, I, J, NT, W, C, PT, NZ = dims
    R = I * J // 128
    JB = J // 128
    s = lax.axis_index("surf")
    w = lax.axis_index("wall")

    cuts = bounds_of(K)
    chunks = len(cuts) - 1

    def flow_copy(c):
        ks = pl.ds(cuts[c], cuts[c + 1] - cuts[c])
        return pltpu.make_async_copy(flow_hbm.at[:, ks], flow.at[:, ks], s_flow.at[c])

    pairs = ((spacing_hbm, spacing), (cells_hbm, cells), (zones_hbm, zones), (abl_hbm, abl),
             (kind_hbm, kind), (conduct_hbm, conduct), (diffuse_hbm, diffuse), (rate_hbm, rate))
    inputs = [pltpu.make_async_copy(a, b, s_in.at[n]) for n, (a, b) in enumerate(pairs)]
    flow_copy(0).start()
    barrier = pltpu.get_barrier_semaphore()
    for d in range(1, NT):
        pl.semaphore_signal(barrier, inc=1, device_id=(lax.rem(s + d, NT), w), device_id_type=MESH)
    for d in range(1, W):
        pl.semaphore_signal(barrier, inc=1, device_id=(s, lax.rem(w + d, W)), device_id_type=MESH)
    for copy in inputs:
        copy.start()
    for c in range(1, chunks):
        flow_copy(c).start()

    def list_copy(d):
        t = lax.rem(s + d, NT)
        return pltpu.make_async_remote_copy(
            send_list.at[t], recv_list.at[d], s_list.at[d], r_list.at[d],
            device_id=(t, w), device_id_type=MESH)

    def total_copy(d):
        return pltpu.make_async_remote_copy(
            slab_total, totals_in.at[w], s_tot.at[d], r_tot.at[d],
            device_id=(s, lax.rem(w + d, W)), device_id_type=MESH)

    def film_copy(d):
        return pltpu.make_async_remote_copy(
            film_buf, film_in, s_film.at[d], r_film,
            device_id=(s, lax.rem(w + d, W)), device_id_type=MESH)

    def halo_copies(side):
        near, target = (K - 2, lax.rem(w + 1, W)) if side == 0 else (0, lax.rem(w + W - 1, W))
        return (
            pltpu.make_async_remote_copy(
                flow_hbm.at[:, near : near + 2], halo_u.at[side], s_hu.at[side], r_hu.at[side],
                device_id=(s, target), device_id_type=MESH),
            pltpu.make_async_remote_copy(
                spacing_hbm.at[near : near + 2], halo_s.at[side], s_hs.at[side], r_hs.at[side],
                device_id=(s, target), device_id_type=MESH),
        )

    def side_copies(c):
        ks = pl.ds(cuts[c], cuts[c + 1] - cuts[c])
        return (
            pltpu.make_async_remote_copy(
                XR.at[ks], RL.at[ks], s_x.at[0, c], r_x.at[0, c],
                device_id=(lax.rem(s + 1, NT), w), device_id_type=MESH),
            pltpu.make_async_remote_copy(
                XL.at[ks], RR.at[ks], s_x.at[1, c], r_x.at[1, c],
                device_id=(lax.rem(s + NT - 1, NT), w), device_id_type=MESH),
        )

    i_row = lax.broadcasted_iota(jnp.int32, (I, J), 0)

    def surface_terms(k, carry):
        u = [flow[e, k] for e in range(5)]
        inv, vx, vy, vz, pressure = primitives_of(*u)
        enthalpy = u[4] + pressure
        sx, sy, sz, sp_ = SCALE * vx, SCALE * vy, SCALE * vz, SCALE * pressure
        m12, m13, m23 = u[1] * sy, u[1] * sz, u[2] * sz
        q = (viscosity * sx, viscosity * sy, viscosity * sz,
             (conduction * inv) * sp_)
        f1 = (SCALE * u[1], u[1] * sx + sp_, m12, m13, enthalpy * sx)
        f2 = (SCALE * u[2], m12, u[2] * sy + sp_, m23, enthalpy * sy)
        f3 = (SCALE * u[3], m13, m23, u[3] * sz + sp_, enthalpy * sz)
        for e in range(5):
            F3[k + 2, e] = f3[e]
        for e in range(4):
            Q[k + 2, e] = q[e]
        for e in range(5):
            total = u[e]
            if e:
                qe = q[e - 1]
                total = total - 60.0 * qe
                q8 = 8.0 * qe
            for axis, size, flux in ((0, I, f1[e]), (1, J, f2[e])):
                if e:
                    up2 = flux - qe
                    down2 = -flux - qe
                    up1 = q8 - 8.0 * up2
                    down1 = q8 - 8.0 * down2
                else:
                    up2 = flux
                    down2 = -flux
                    up1 = -8.0 * flux
                    down1 = 8.0 * flux
                r1 = pltpu.roll(down1, 1, axis)
                r2 = pltpu.roll(down2, 2, axis)
                l1 = pltpu.roll(up1, size - 1, axis)
                l2 = pltpu.roll(up2, size - 2, axis)
                if axis == 0:
                    to_right = r2 + jnp.where(i_row == 0, r1, 0.0)
                    to_left = up2 + jnp.where(i_row == 1, pltpu.roll(up1, 1, 0), 0.0)
                    XR[k, e] = to_right[0:2]
                    XL[k, e] = to_left[0:2]
                    r1 = jnp.where(i_row >= 1, r1, 0.0)
                    r2 = jnp.where(i_row >= 2, r2, 0.0)
                    l1 = jnp.where(i_row <= I - 2, l1, 0.0)
                    l2 = jnp.where(i_row <= I - 3, l2, 0.0)
                total = total + ((r1 + r2) + (l1 + l2))
            out[e, k] = total
        return carry

    def chunk(c, send=True):
        flow_copy(c).wait()
        lax.fori_loop(cuts[c], cuts[c + 1], surface_terms, 0)
        if send:
            for copy in side_copies(c):
                copy.start()

    chunk(0, send=False)
    pl.semaphore_wait(barrier, NT - 1 + W - 1)
    for copy in side_copies(0):
        copy.start()
    @pl.when(w < W - 1)
    def _():
        for copy in halo_copies(0):
            copy.start()

    @pl.when(w > 0)
    def _():
        for copy in halo_copies(1):
            copy.start()

    chunk(1)
    inputs[0].wait()
    def add_total(k, total):
        layer = spacing[k]
        sp[k + 2] = layer
        return total + layer

    slab_total[...] = lax.fori_loop(0, K, add_total, jnp.zeros((I, J), f32))
    inv, vx, vy, vz, pressure = primitives_of(*[flow[e, 0] for e in range(5)])
    film_buf[0] = 2.0 / spacing[0]
    film_buf[1] = pressure * inv + 0.2 * (vx * vx + vy * vy + vz * vz)

    @pl.when(w == 0)
    def _():
        for d in range(1, W):
            film_copy(d).start()

    for d in range(1, W):
        total_copy(d).start()
    totals_in[w] = slab_total[...]

    for c in (2, 3, 4):
        chunk(c)

    for copy in inputs[1:]:
        copy.wait()
    cell = cells[...]
    tile = lax.shift_right_logical(cell, shift_of(I * J))
    within = jnp.bitwise_and(cell, I * J - 1)
    row_i = lax.shift_right_logical(within, shift_of(J))
    col_j = jnp.bitwise_and(within, J - 1)
    row = lax.shift_right_logical(col_j, 7) * I + row_i
    lane = jnp.bitwise_and(col_j, 127)
    zone = zones[...]
    tile_iota = lax.broadcasted_iota(jnp.int32, (NT, C), 0)
    lane_iota = lax.broadcasted_iota(jnp.int32, (NT, C), 1)
    mine = jnp.where(tile_iota == tile, 1.0, 0.0).astype(f32)
    run = mine
    step = 1
    while step < C:
        run = run + jnp.where(lane_iota >= step, pltpu.roll(run, step, 1), 0.0)
        step *= 2
    rank = jnp.sum(mine * run, axis=0, keepdims=True).astype(jnp.int32) - 1
    slot = tile * PT + rank
    V[...] = jnp.zeros(V.shape, f32)
    V[0:1, 0:C] = row.astype(f32)
    V[1:2, 0:C] = lane.astype(f32)
    V[2:3, 0:C] = zone.astype(f32)
    for n, piece in enumerate(parts3(abl[0:1, :]) + parts3(abl[1:2, :])):
        V[3 + n : 4 + n, 0:C] = piece
    payload = V[:, 0:C].astype(bf16)
    slot_iota = lax.broadcasted_iota(jnp.int32, (PT, C), 0)
    for t in range(NT):
        block = jnp.where(slot_iota + t * PT == slot, 1.0, 0.0).astype(bf16)
        PM[t * PT : (t + 1) * PT, :] = block
        got = lax.dot_general(payload, block, (((1,), (1,)), ((), ())), preferred_element_type=f32)
        send_list[t] = jnp.zeros((8, PT), f32)
        send_list[t, 0:3] = got[0:3]
        send_list[t, 3:4] = got[3:4] + got[4:5] + got[5:6]
        send_list[t, 4:5] = got[6:7] + got[7:8] + got[8:9]

    for d in range(1, NT):
        list_copy(d).start()

    for c in (5, 6):
        chunk(c)

    recv_list[0] = send_list[s]
    for d in range(1, NT):
        list_copy(d).wait()
    listed = jnp.concatenate([recv_list[d] for d in range(NT)], axis=1)
    count = NT * PT
    l_row = listed[0:1].astype(jnp.int32)
    l_lane = listed[1:2].astype(jnp.int32)
    row_hot = jnp.where(lax.broadcasted_iota(jnp.int32, (R, count), 0) == l_row, 1.0, 0.0)
    lane_hot = jnp.where(
        lax.broadcasted_iota(jnp.int32, (128, count), 0) == l_lane, 1.0, 0.0).astype(bf16)
    pieces = parts3(listed[3:4]) + parts3(listed[4:5]) + (listed[2:3],)
    stack = jnp.concatenate([row_hot * piece for piece in pieces], axis=0).astype(bf16)
    grid = lax.dot_general(stack, lane_hot, (((1,), (1,)), ((), ())), preferred_element_type=f32)
    first = grid[0:R] + grid[R : 2 * R] + grid[2 * R : 3 * R]
    second = grid[3 * R : 4 * R] + grid[4 * R : 5 * R] + grid[5 * R : 6 * R]
    zone_grid = grid[6 * R : 7 * R]

    @pl.when(w == 0)
    def _():
        for d in range(1, W):
            film_copy(d).wait_send()
        film_in[...] = film_buf[...]

    @pl.when(w > 0)
    def _():
        film_copy(1).wait_recv()

    film = jnp.concatenate([film_in[0, :, b * 128 : (b + 1) * 128] for b in range(JB)], axis=0)
    recov = jnp.concatenate([film_in[1, :, b * 128 : (b + 1) * 128] for b in range(JB)], axis=0)
    zone_grid = zone_grid.astype(jnp.int32)
    owned = first > 0.25
    cond = pick(zone_grid, conduct, NZ)
    surface = jnp.where(owned, first, 1.0)
    for newton_pass in range(2):
        cube = surface * surface * surface
        surface = (film * recov + cond * second + 2.4 * cube * surface) / (film + cond + 3.2 * cube)
    recess = pick(zone_grid, rate, NZ) * jnp.exp(-2.0 / surface)
    part[0] = jnp.where(owned, surface, 0.0)
    part[1] = jnp.where(owned, recess, 0.0)

    def part_copy(d):
        return pltpu.make_async_remote_copy(
            part, part_in.at[d], s_part.at[d], r_part.at[d],
            device_id=(s, lax.rem(w + d, W)), device_id_type=MESH)

    for d in range(1, W):
        part_copy(d).start()

    table = jnp.concatenate(parts3(part[0]), axis=0).astype(bf16)
    spread = jnp.dot(table, lane_hot, preferred_element_type=f32)
    spread = spread[0:R] + spread[R : 2 * R] + spread[2 * R : 3 * R]
    answer = jnp.sum(spread * row_hot, axis=0, keepdims=True)
    for d in range(NT):
        reply[d] = jnp.broadcast_to(answer[:, d * PT : (d + 1) * PT], (8, PT))

    def reply_copy(d):
        return pltpu.make_async_remote_copy(
            reply.at[d], reply_in.at[s], s_rep.at[d], r_rep.at[d],
            device_id=(lax.rem(s + NT - d, NT), w), device_id_type=MESH)

    for d in range(1, NT):
        reply_copy(d).start()
    reply_in[s] = reply[0]
    for c in range(7, chunks):
        chunk(c)

    for d in range(1, W):
        part_copy(d).wait()
    whole = part[...]
    for d in range(1, W):
        whole = whole + part_in[d]
    dense[...] = whole
    surf_temp = jnp.concatenate([dense[0, b * I : (b + 1) * I, :] for b in range(JB)], axis=1)
    surf_recess = jnp.concatenate([dense[1, b * I : (b + 1) * I, :] for b in range(JB)], axis=1)

    for d in range(1, W):
        total_copy(d).wait()
    column_total = jnp.zeros((I, J), f32)
    offset = jnp.zeros((I, J), f32)
    for n in range(W):
        column_total = column_total + totals_in[n]
        offset = offset + jnp.where(n < w, totals_in[n], 0.0)

    @pl.when(w < W - 1)
    def _():
        for copy in halo_copies(0):
            copy.wait_send()
        for copy in halo_copies(1):
            copy.wait_recv()

    @pl.when(w > 0)
    def _():
        for copy in halo_copies(1):
            copy.wait_send()
        for copy in halo_copies(0):
            copy.wait_recv()

    def put(at, values):
        flux, fields = values
        for e in range(5):
            F3[at, e] = flux[e]
        for e in range(4):
            Q[at, e] = fields[e]

    def put_halo(side, base):
        for n in range(2):
            u = [halo_u[side, e, n] for e in range(5)]
            inv, vx, vy, vz, pressure = primitives_of(*u)
            put(base + n, normal_fields(u[0], vx, vy, vz, pressure))
            sp[base + n] = halo_s[side, n]

    @pl.when(w > 0)
    def _():
        put_halo(0, 0)

    @pl.when(w < W - 1)
    def _():
        put_halo(1, K + 2)

    @pl.when(w == 0)
    def _():
        kinds = kind[...]
        slip = kinds == 1
        for n in range(2):
            u = [flow[e, n] for e in range(5)]
            inv, vx, vy, vz, pressure = primitives_of(*u)
            density = jnp.where(slip, u[0], pressure / surf_temp)
            vx = jnp.where(slip, vx, -vx)
            vy = jnp.where(slip, vy, -vy)
            vz = jnp.where(kinds == 2, 2.0 * surf_recess - vz, -vz)
            put(1 - n, normal_fields(density, vx, vy, vz, pressure))
        sp[1] = spacing[1]
        sp[0] = spacing[0]

    @pl.when(w == W - 1)
    def _():
        one = jnp.full((I, J), 1.0, f32)
        zero = jnp.zeros((I, J), f32)
        for n in range(2):
            put(K + 2 + n, normal_fields(one, 0.5 * one, zero, zero, one))
        sp[K + 2] = spacing[K - 2]
        sp[K + 3] = spacing[K - 1]

    inv_total = 1.0 / column_total
    stretch = (1.0 + surf_recess * inv_total) * (1.0 / 12.0)

    def normal_terms(k, run):
        here = sp[k + 2]
        metric = stretch * (
            3.0 * (sp[k + 1] + sp[k + 3]) + 7.0 * here - 0.5 * (sp[k] + sp[k + 4]))
        inv_metric = 1.0 / metric
        inv_square = inv_metric * inv_metric
        normalized = (run + 0.5 * here) * inv_total
        shift_out[k] = surf_recess * (normalized - 1.0)
        damp = (time_step * sponge_rate) * normalized * normalized
        for e in range(5):
            diff = 8.0 * (F3[k + 3, e] - F3[k + 1, e]) - (F3[k + 4, e] - F3[k, e])
            total = out[e, k] - inv_metric * diff - damp * (flow[e, k] - far_values[e])
            if e:
                lap = (16.0 * (Q[k + 3, e - 1] + Q[k + 1, e - 1])
                       - (Q[k + 4, e - 1] + Q[k, e - 1]) - 30.0 * Q[k + 2, e - 1])
                total = total + inv_square * lap
            out[e, k] = total
        return run + here

    lax.fori_loop(0, K, normal_terms, offset)

    for d in range(1, NT):
        reply_copy(d).wait()
    answer = jnp.concatenate([reply_in[t, 0:1] for t in range(NT)], axis=1)
    V[...] = jnp.zeros(V.shape, f32)
    for n, piece in enumerate(parts3(answer)):
        V[n : n + 1, 0:count] = piece
    back = jnp.dot(V[:, 0:count].astype(bf16), PM[...], preferred_element_type=f32)
    col_surface = back[0:1] + back[1:2] + back[2:3]
    col_diffuse = pick(zone, diffuse, NZ)
    depth = abl.shape[0]
    depth_row = lax.broadcasted_iota(jnp.int32, (depth, C), 0)
    profile = jnp.where(depth_row == 0, col_surface, abl[...])
    for heat_pass in range(2):
        below = pltpu.roll(profile, 1, 0)
        above = jnp.where(depth_row == depth - 1, below, pltpu.roll(profile, depth - 1, 0))
        gain = col_diffuse * (above - 2.0 * profile + below)
        profile = jnp.where(depth_row == 0, profile, profile + gain)
    abl_out[...] = profile

    for c in range(chunks):
        for copy in side_copies(c):
            copy.wait()


def hand_out(state_in, shift, abl, RL, RR, state_hbm, shift_hbm, abl_hbm, state, s_out):
    K, I, J = state.shape[1:]
    size = K // HAND

    def store(c):
        ks = pl.ds(c * size, size)
        return pltpu.make_async_copy(state.at[:, ks], state_hbm.at[:, ks], s_out.at[c])

    def add_sides(k, carry):
        for e in range(5):
            middle = jnp.zeros((I - 4, J), f32)
            state[e, k] = state_in[e, k] + jnp.concatenate([RL[k, e], middle, RR[k, e]], axis=0)
        return carry

    rest = (pltpu.make_async_copy(shift, shift_hbm, s_out.at[HAND]),
            pltpu.make_async_copy(abl, abl_hbm, s_out.at[HAND + 1]))
    for copy in rest:
        copy.start()
    for c in range(HAND):
        lax.fori_loop(c * size, (c + 1) * size, add_sides, 0)
        store(c).start()
    for c in range(HAND):
        store(c).wait()
    for copy in rest:
        copy.wait()


def shards(flow_state, spacing, bc_kind, cell_of, zone_id, abl_temp, conduct, diffuse, rate):
    NT = lax.axis_size("surf")
    W = lax.axis_size("wall")
    K, I, J = spacing.shape
    C = cell_of.shape[0]
    PT = -(-(C // NT) // 128) * 128
    R = I * J // 128
    count = NT * PT
    dims = (K, I, J, NT, W, C, PT, conduct.shape[0])
    dma = pltpu.SemaphoreType.DMA
    chunks = len(bounds_of(K)) - 1
    scratch = [
        pltpu.VMEM(flow_state.shape, f32),
        pltpu.VMEM(spacing.shape, f32),
        pltpu.VMEM(bc_kind.shape, jnp.int32),
        pltpu.VMEM((1, C), jnp.int32),
        pltpu.VMEM((1, C), jnp.int32),
        pltpu.VMEM(abl_temp.shape, f32),
        pltpu.SMEM(conduct.shape, f32),
        pltpu.SMEM(conduct.shape, f32),
        pltpu.SMEM(conduct.shape, f32),
        dma((chunks,)), dma((8,)),
        pltpu.VMEM((K + 4, 5, I, J), f32),
        pltpu.VMEM((K + 4, 4, I, J), f32),
        pltpu.VMEM((K, 5, 2, J), f32),
        pltpu.VMEM((K, 5, 2, J), f32),
        pltpu.VMEM((count, C), bf16),
        pltpu.VMEM((16, max(C, count)), f32),
        pltpu.VMEM((NT, 8, PT), f32),
        pltpu.VMEM((NT, 8, PT), f32),
        pltpu.VMEM((NT, 8, PT), f32),
        pltpu.VMEM((NT, 8, PT), f32),
        pltpu.VMEM((I, J), f32),
        pltpu.VMEM((W, I, J), f32),
        pltpu.VMEM((2, I, J), f32),
        pltpu.VMEM((2, I, J), f32),
        pltpu.VMEM((2, R, 128), f32),
        pltpu.VMEM((W, 2, R, 128), f32),
        pltpu.VMEM((2, 5, 2, I, J), f32),
        pltpu.VMEM((2, 2, I, J), f32),
        pltpu.VMEM((K + 4, I, J), f32),
        pltpu.VMEM((2, R, 128), f32),
        dma((NT,)), dma((NT,)), dma((NT,)), dma((NT,)),
        dma((W,)), dma((W,)), dma((W,)), dma,
        dma((W,)), dma((W,)),
        dma((2,)), dma((2,)), dma((2,)), dma((2,)),
        dma((2, chunks)), dma((2, chunks)),
    ]
    hbm = pl.BlockSpec(memory_space=pltpu.HBM)
    vmem = pl.BlockSpec(memory_space=pltpu.VMEM)
    held = [pltpu.with_memory_space_constraint(x, pltpu.HBM) for x in (
        flow_state, spacing, bc_kind, cell_of.reshape(1, C), zone_id.reshape(1, C), abl_temp,
        conduct, diffuse, rate)]
    results = pl.pallas_call(
        functools.partial(kernel, dims),
        out_shape=(
            jax.ShapeDtypeStruct(flow_state.shape, f32),
            jax.ShapeDtypeStruct(spacing.shape, f32),
            jax.ShapeDtypeStruct(abl_temp.shape, f32),
            jax.ShapeDtypeStruct((K, 5, 2, J), f32),
            jax.ShapeDtypeStruct((K, 5, 2, J), f32),
        ),
        in_specs=[hbm] * 9,
        out_specs=(vmem,) * 5,
        scratch_shapes=scratch,
        compiler_params=pltpu.CompilerParams(
            collective_id=0, has_side_effects=True, vmem_limit_bytes=VMEM_BYTES),
    )(*held)
    return pl.pallas_call(
        hand_out,
        out_shape=[jax.ShapeDtypeStruct(r.shape, f32) for r in results[:3]],
        in_specs=[vmem] * 5,
        out_specs=[hbm] * 3,
        scratch_shapes=[pltpu.VMEM(flow_state.shape, f32), dma((HAND + 2,))],
        compiler_params=pltpu.CompilerParams(vmem_limit_bytes=VMEM_BYTES),
    )(*results)


def solution(mesh):
    in_specs = (
        P(None, "wall", "surf", None),
        P("wall", "surf", None),
        P("surf", None),
        P(("surf", "wall")),
        P(("surf", "wall")),
        P(None, ("surf", "wall")),
        P(),
        P(),
        P(),
    )
    out_specs = (P(None, "wall", "surf", None), P("wall", "surf", None), P(None, ("surf", "wall")))
    return jax.shard_map(shards, mesh=mesh, in_specs=in_specs, out_specs=out_specs, check_vma=False)
```

```python
import functools

import jax
import jax.numpy as jnp
from jax import lax
from jax.experimental import pallas as pl
from jax.experimental.pallas import tpu as pltpu
from jax.sharding import PartitionSpec as P

f32 = jnp.float32
bf16 = jnp.bfloat16
MESH = pl.DeviceIdType.MESH

time_step = 0.15
viscosity = 0.05
conduction = 0.07
sponge_rate = 0.5
far_values = (1.0, 0.5, 0.0, 0.0, 2.625)
SCALE = time_step / 12.0
CHUNK = 4
HAND = 4
VMEM_BYTES = 26 * 1024 * 1024


def bounds_of(K):
    return (0, 2) + tuple(range(4, K + 1, CHUNK))


def parts3(x):
    a = x.astype(bf16).astype(f32)
    b = (x - a).astype(bf16).astype(f32)
    c = (x - a - b).astype(bf16).astype(f32)
    return a, b, c


def shift_of(n):
    assert n & (n - 1) == 0
    return n.bit_length() - 1


def pick(index, table_ref, count):
    out = jnp.zeros(index.shape, f32)
    for z in range(count):
        out = jnp.where(index == z, table_ref[z], out)
    return out


def normal_fields(density, vx, vy, vz, pressure):
    energy = 2.5 * pressure + 0.5 * density * (vx * vx + vy * vy + vz * vz)
    svz = SCALE * vz
    rho_w = density * svz
    flux = (
        rho_w,
        rho_w * vx,
        rho_w * vy,
        rho_w * vz + SCALE * pressure,
        (energy + pressure) * svz,
    )
    cv = SCALE * viscosity
    return flux, (cv * vx, cv * vy, cv * vz, (SCALE * conduction) * (pressure / density))


def primitives_of(u0, u1, u2, u3, u4):
    inv = 1.0 / u0
    vx, vy, vz = u1 * inv, u2 * inv, u3 * inv
    pressure = 0.4 * (u4 - 0.5 * (u1 * vx + u2 * vy + u3 * vz))
    return inv, vx, vy, vz, pressure


def kernel(
    dims,
    flow_hbm, spacing_hbm, kind_hbm, cells_hbm, zones_hbm, abl_hbm, conduct_hbm, diffuse_hbm, rate_hbm,
    out, shift_out, abl_out, RL, RR,
    flow, spacing, kind, cells, zones, abl, conduct, diffuse, rate, s_flow, s_in,
    F3, Q, XR, XL, PM, V, send_list, recv_list, reply, reply_in,
    slab_total, totals_in, film_buf, film_in, part, part_in,
    halo_u, halo_s, sp, dense,
    s_list, r_list, s_rep, r_rep, s_tot, r_tot, s_film, r_film, s_part, r_part,
    s_hu, r_hu, s_hs, r_hs, s_x, r_x,
):
    K, I, J, NT, W, C, PT, NZ = dims
    R = I * J // 128
    JB = J // 128
    s = lax.axis_index("surf")
    w = lax.axis_index("wall")

    cuts = bounds_of(K)
    chunks = len(cuts) - 1

    def flow_copy(c):
        ks = pl.ds(cuts[c], cuts[c + 1] - cuts[c])
        return pltpu.make_async_copy(flow_hbm.at[:, ks], flow.at[:, ks], s_flow.at[c])

    pairs = ((spacing_hbm, spacing), (cells_hbm, cells), (zones_hbm, zones), (abl_hbm, abl),
             (kind_hbm, kind), (conduct_hbm, conduct), (diffuse_hbm, diffuse), (rate_hbm, rate))
    inputs = [pltpu.make_async_copy(a, b, s_in.at[n]) for n, (a, b) in enumerate(pairs)]
    flow_copy(0).start()
    barrier = pltpu.get_barrier_semaphore()
    for d in range(1, NT):
        pl.semaphore_signal(barrier, inc=1, device_id=(lax.rem(s + d, NT), w), device_id_type=MESH)
    for d in range(1, W):
        pl.semaphore_signal(barrier, inc=1, device_id=(s, lax.rem(w + d, W)), device_id_type=MESH)
    for copy in inputs:
        copy.start()
    for c in range(1, chunks):
        flow_copy(c).start()

    def list_copy(d):
        t = lax.rem(s + d, NT)
        return pltpu.make_async_remote_copy(
            send_list.at[t], recv_list.at[d], s_list.at[d], r_list.at[d],
            device_id=(t, w), device_id_type=MESH)

    def total_copy(d):
        return pltpu.make_async_remote_copy(
            slab_total, totals_in.at[w], s_tot.at[d], r_tot.at[d],
            device_id=(s, lax.rem(w + d, W)), device_id_type=MESH)

    def film_copy(d):
        return pltpu.make_async_remote_copy(
            film_buf, film_in, s_film.at[d], r_film,
            device_id=(s, lax.rem(w + d, W)), device_id_type=MESH)

    def halo_copies(side):
        near, target = (K - 2, lax.rem(w + 1, W)) if side == 0 else (0, lax.rem(w + W - 1, W))
        return (
            pltpu.make_async_remote_copy(
                flow_hbm.at[:, near : near + 2], halo_u.at[side], s_hu.at[side], r_hu.at[side],
                device_id=(s, target), device_id_type=MESH),
            pltpu.make_async_remote_copy(
                spacing_hbm.at[near : near + 2], halo_s.at[side], s_hs.at[side], r_hs.at[side],
                device_id=(s, target), device_id_type=MESH),
        )

    def side_copies(c):
        ks = pl.ds(cuts[c], cuts[c + 1] - cuts[c])
        return (
            pltpu.make_async_remote_copy(
                XR.at[ks], RL.at[ks], s_x.at[0, c], r_x.at[0, c],
                device_id=(lax.rem(s + 1, NT), w), device_id_type=MESH),
            pltpu.make_async_remote_copy(
                XL.at[ks], RR.at[ks], s_x.at[1, c], r_x.at[1, c],
                device_id=(lax.rem(s + NT - 1, NT), w), device_id_type=MESH),
        )

    i_row = lax.broadcasted_iota(jnp.int32, (I, J), 0)

    def surface_terms(k, carry):
        u = [flow[e, k] for e in range(5)]
        inv, vx, vy, vz, pressure = primitives_of(*u)
        enthalpy = u[4] + pressure
        sx, sy, sz, sp_ = SCALE * vx, SCALE * vy, SCALE * vz, SCALE * pressure
        m12, m13, m23 = u[1] * sy, u[1] * sz, u[2] * sz
        q = (viscosity * sx, viscosity * sy, viscosity * sz,
             (conduction * inv) * sp_)
        f1 = (SCALE * u[1], u[1] * sx + sp_, m12, m13, enthalpy * sx)
        f2 = (SCALE * u[2], m12, u[2] * sy + sp_, m23, enthalpy * sy)
        f3 = (SCALE * u[3], m13, m23, u[3] * sz + sp_, enthalpy * sz)
        for e in range(5):
            F3[k + 2, e] = f3[e]
        for e in range(4):
            Q[k + 2, e] = q[e]
        for e in range(5):
            total = u[e]
            if e:
                qe = q[e - 1]
                total = total - 60.0 * qe
                q8 = 8.0 * qe
            for axis, size, flux in ((0, I, f1[e]), (1, J, f2[e])):
                if e:
                    up2 = flux - qe
                    down2 = -flux - qe
                    up1 = q8 - 8.0 * up2
                    down1 = q8 - 8.0 * down2
                else:
                    up2 = flux
                    down2 = -flux
                    up1 = -8.0 * flux
                    down1 = 8.0 * flux
                r1 = pltpu.roll(down1, 1, axis)
                r2 = pltpu.roll(down2, 2, axis)
                l1 = pltpu.roll(up1, size - 1, axis)
                l2 = pltpu.roll(up2, size - 2, axis)
                if axis == 0:
                    to_right = r2 + jnp.where(i_row == 0, r1, 0.0)
                    to_left = up2 + jnp.where(i_row == 1, pltpu.roll(up1, 1, 0), 0.0)
                    XR[k, e] = to_right[0:2]
                    XL[k, e] = to_left[0:2]
                    r1 = jnp.where(i_row >= 1, r1, 0.0)
                    r2 = jnp.where(i_row >= 2, r2, 0.0)
                    l1 = jnp.where(i_row <= I - 2, l1, 0.0)
                    l2 = jnp.where(i_row <= I - 3, l2, 0.0)
                total = total + ((r1 + r2) + (l1 + l2))
            out[e, k] = total
        return carry

    def chunk(c, send=True):
        flow_copy(c).wait()
        lax.fori_loop(cuts[c], cuts[c + 1], surface_terms, 0)
        if send:
            for copy in side_copies(c):
                copy.start()

    chunk(0, send=False)
    pl.semaphore_wait(barrier, NT - 1 + W - 1)
    for copy in side_copies(0):
        copy.start()
    @pl.when(w < W - 1)
    def _():
        for copy in halo_copies(0):
            copy.start()

    @pl.when(w > 0)
    def _():
        for copy in halo_copies(1):
            copy.start()

    chunk(1)
    chunk(2)

    for copy in inputs[1:]:
        copy.wait()
    cell = cells[...]
    tile = lax.shift_right_logical(cell, shift_of(I * J))
    within = jnp.bitwise_and(cell, I * J - 1)
    row_i = lax.shift_right_logical(within, shift_of(J))
    col_j = jnp.bitwise_and(within, J - 1)
    row = lax.shift_right_logical(col_j, 7) * I + row_i
    lane = jnp.bitwise_and(col_j, 127)
    zone = zones[...]
    tile_iota = lax.broadcasted_iota(jnp.int32, (NT, C), 0)
    lane_iota = lax.broadcasted_iota(jnp.int32, (NT, C), 1)
    mine = jnp.where(tile_iota == tile, 1.0, 0.0).astype(f32)
    run = mine
    step = 1
    while step < C:
        run = run + jnp.where(lane_iota >= step, pltpu.roll(run, step, 1), 0.0)
        step *= 2
    rank = jnp.sum(mine * run, axis=0, keepdims=True).astype(jnp.int32) - 1
    slot = tile * PT + rank
    V[...] = jnp.zeros(V.shape, f32)
    V[0:1, 0:C] = row.astype(f32)
    V[1:2, 0:C] = lane.astype(f32)
    V[2:3, 0:C] = zone.astype(f32)
    for n, piece in enumerate(parts3(abl[0:1, :]) + parts3(abl[1:2, :])):
        V[3 + n : 4 + n, 0:C] = piece
    payload = V[:, 0:C].astype(bf16)
    slot_iota = lax.broadcasted_iota(jnp.int32, (PT, C), 0)
    for t in range(NT):
        block = jnp.where(slot_iota + t * PT == slot, 1.0, 0.0).astype(bf16)
        PM[t * PT : (t + 1) * PT, :] = block
        got = lax.dot_general(payload, block, (((1,), (1,)), ((), ())), preferred_element_type=f32)
        send_list[t] = jnp.zeros((8, PT), f32)
        send_list[t, 0:3] = got[0:3]
        send_list[t, 3:4] = got[3:4] + got[4:5] + got[5:6]
        send_list[t, 4:5] = got[6:7] + got[7:8] + got[8:9]

    for d in range(1, NT):
        list_copy(d).start()

    inputs[0].wait()
    def add_total(k, total):
        layer = spacing[k]
        sp[k + 2] = layer
        return total + layer

    slab_total[...] = lax.fori_loop(0, K, add_total, jnp.zeros((I, J), f32))
    inv, vx, vy, vz, pressure = primitives_of(*[flow[e, 0] for e in range(5)])
    film_buf[0] = 2.0 / spacing[0]
    film_buf[1] = pressure * inv + 0.2 * (vx * vx + vy * vy + vz * vz)

    @pl.when(w == 0)
    def _():
        for d in range(1, W):
            film_copy(d).start()

    for d in range(1, W):
        total_copy(d).start()
    totals_in[w] = slab_total[...]

    for c in (3, 4, 5):
        chunk(c)

    recv_list[0] = send_list[s]
    for d in range(1, NT):
        list_copy(d).wait()
    listed = jnp.concatenate([recv_list[d] for d in range(NT)], axis=1)
    count = NT * PT
    l_row = listed[0:1].astype(jnp.int32)
    l_lane = listed[1:2].astype(jnp.int32)
    row_hot = jnp.where(lax.broadcasted_iota(jnp.int32, (R, count), 0) == l_row, 1.0, 0.0)
    lane_hot = jnp.where(
        lax.broadcasted_iota(jnp.int32, (128, count), 0) == l_lane, 1.0, 0.0).astype(bf16)
    pieces = parts3(listed[3:4]) + parts3(listed[4:5]) + (listed[2:3],)
    stack = jnp.concatenate([row_hot * piece for piece in pieces], axis=0).astype(bf16)
    grid = lax.dot_general(stack, lane_hot, (((1,), (1,)), ((), ())), preferred_element_type=f32)
    first = grid[0:R] + grid[R : 2 * R] + grid[2 * R : 3 * R]
    second = grid[3 * R : 4 * R] + grid[4 * R : 5 * R] + grid[5 * R : 6 * R]
    zone_grid = grid[6 * R : 7 * R]

    @pl.when(w == 0)
    def _():
        for d in range(1, W):
            film_copy(d).wait_send()
        film_in[...] = film_buf[...]

    @pl.when(w > 0)
    def _():
        film_copy(1).wait_recv()

    film = jnp.concatenate([film_in[0, :, b * 128 : (b + 1) * 128] for b in range(JB)], axis=0)
    recov = jnp.concatenate([film_in[1, :, b * 128 : (b + 1) * 128] for b in range(JB)], axis=0)
    zone_grid = zone_grid.astype(jnp.int32)
    owned = first > 0.25
    cond = pick(zone_grid, conduct, NZ)
    surface = jnp.where(owned, first, 1.0)
    for newton_pass in range(2):
        cube = surface * surface * surface
        surface = (film * recov + cond * second + 2.4 * cube * surface) / (film + cond + 3.2 * cube)
    recess = pick(zone_grid, rate, NZ) * jnp.exp(-2.0 / surface)
    part[0] = jnp.where(owned, surface, 0.0)
    part[1] = jnp.where(owned, recess, 0.0)

    def part_copy(d):
        return pltpu.make_async_remote_copy(
            part, part_in.at[d], s_part.at[d], r_part.at[d],
            device_id=(s, lax.rem(w + d, W)), device_id_type=MESH)

    for d in range(1, W):
        part_copy(d).start()

    table = jnp.concatenate(parts3(part[0]), axis=0).astype(bf16)
    spread = jnp.dot(table, lane_hot, preferred_element_type=f32)
    spread = spread[0:R] + spread[R : 2 * R] + spread[2 * R : 3 * R]
    answer = jnp.sum(spread * row_hot, axis=0, keepdims=True)
    for d in range(NT):
        reply[d] = jnp.broadcast_to(answer[:, d * PT : (d + 1) * PT], (8, PT))

    def reply_copy(d):
        return pltpu.make_async_remote_copy(
            reply.at[d], reply_in.at[s], s_rep.at[d], r_rep.at[d],
            device_id=(lax.rem(s + NT - d, NT), w), device_id_type=MESH)

    for d in range(1, NT):
        reply_copy(d).start()
    reply_in[s] = reply[0]
    for c in range(6, chunks):
        chunk(c)

    for d in range(1, NT):
        reply_copy(d).wait()
    answer = jnp.concatenate([reply_in[t, 0:1] for t in range(NT)], axis=1)
    V[...] = jnp.zeros(V.shape, f32)
    for n, piece in enumerate(parts3(answer)):
        V[n : n + 1, 0:count] = piece
    back = jnp.dot(V[:, 0:count].astype(bf16), PM[...], preferred_element_type=f32)
    col_surface = back[0:1] + back[1:2] + back[2:3]
    col_diffuse = pick(zone, diffuse, NZ)
    depth = abl.shape[0]
    depth_row = lax.broadcasted_iota(jnp.int32, (depth, C), 0)
    profile = jnp.where(depth_row == 0, col_surface, abl[...])
    for heat_pass in range(2):
        below = pltpu.roll(profile, 1, 0)
        above = jnp.where(depth_row == depth - 1, below, pltpu.roll(profile, depth - 1, 0))
        gain = col_diffuse * (above - 2.0 * profile + below)
        profile = jnp.where(depth_row == 0, profile, profile + gain)
    abl_out[...] = profile

    for d in range(1, W):
        part_copy(d).wait()
    whole = part[...]
    for d in range(1, W):
        whole = whole + part_in[d]
    dense[...] = whole
    surf_temp = jnp.concatenate([dense[0, b * I : (b + 1) * I, :] for b in range(JB)], axis=1)
    surf_recess = jnp.concatenate([dense[1, b * I : (b + 1) * I, :] for b in range(JB)], axis=1)

    for d in range(1, W):
        total_copy(d).wait()
    column_total = jnp.zeros((I, J), f32)
    offset = jnp.zeros((I, J), f32)
    for n in range(W):
        column_total = column_total + totals_in[n]
        offset = offset + jnp.where(n < w, totals_in[n], 0.0)

    @pl.when(w < W - 1)
    def _():
        for copy in halo_copies(0):
            copy.wait_send()
        for copy in halo_copies(1):
            copy.wait_recv()

    @pl.when(w > 0)
    def _():
        for copy in halo_copies(1):
            copy.wait_send()
        for copy in halo_copies(0):
            copy.wait_recv()

    def put(at, values):
        flux, fields = values
        for e in range(5):
            F3[at, e] = flux[e]
        for e in range(4):
            Q[at, e] = fields[e]

    def put_halo(side, base):
        for n in range(2):
            u = [halo_u[side, e, n] for e in range(5)]
            inv, vx, vy, vz, pressure = primitives_of(*u)
            put(base + n, normal_fields(u[0], vx, vy, vz, pressure))
            sp[base + n] = halo_s[side, n]

    @pl.when(w > 0)
    def _():
        put_halo(0, 0)

    @pl.when(w < W - 1)
    def _():
        put_halo(1, K + 2)

    @pl.when(w == 0)
    def _():
        kinds = kind[...]
        slip = kinds == 1
        for n in range(2):
            u = [flow[e, n] for e in range(5)]
            inv, vx, vy, vz, pressure = primitives_of(*u)
            density = jnp.where(slip, u[0], pressure / surf_temp)
            vx = jnp.where(slip, vx, -vx)
            vy = jnp.where(slip, vy, -vy)
            vz = jnp.where(kinds == 2, 2.0 * surf_recess - vz, -vz)
            put(1 - n, normal_fields(density, vx, vy, vz, pressure))
        sp[1] = spacing[1]
        sp[0] = spacing[0]

    @pl.when(w == W - 1)
    def _():
        one = jnp.full((I, J), 1.0, f32)
        zero = jnp.zeros((I, J), f32)
        for n in range(2):
            put(K + 2 + n, normal_fields(one, 0.5 * one, zero, zero, one))
        sp[K + 2] = spacing[K - 2]
        sp[K + 3] = spacing[K - 1]

    inv_total = 1.0 / column_total
    stretch = (1.0 + surf_recess * inv_total) * (1.0 / 12.0)

    def normal_terms(k, run):
        here = sp[k + 2]
        metric = stretch * (
            3.0 * (sp[k + 1] + sp[k + 3]) + 7.0 * here - 0.5 * (sp[k] + sp[k + 4]))
        inv_metric = 1.0 / metric
        inv_square = inv_metric * inv_metric
        normalized = (run + 0.5 * here) * inv_total
        shift_out[k] = surf_recess * (normalized - 1.0)
        damp = (time_step * sponge_rate) * normalized * normalized
        for e in range(5):
            diff = 8.0 * (F3[k + 3, e] - F3[k + 1, e]) - (F3[k + 4, e] - F3[k, e])
            total = out[e, k] - inv_metric * diff - damp * (flow[e, k] - far_values[e])
            if e:
                lap = (16.0 * (Q[k + 3, e - 1] + Q[k + 1, e - 1])
                       - (Q[k + 4, e - 1] + Q[k, e - 1]) - 30.0 * Q[k + 2, e - 1])
                total = total + inv_square * lap
            out[e, k] = total
        return run + here

    lax.fori_loop(0, K, normal_terms, offset)

    for c in range(chunks):
        for copy in side_copies(c):
            copy.wait()


def hand_out(state_in, shift, abl, RL, RR, state_hbm, shift_hbm, abl_hbm, state, s_out):
    K, I, J = state.shape[1:]
    size = K // HAND

    def store(c):
        ks = pl.ds(c * size, size)
        return pltpu.make_async_copy(state.at[:, ks], state_hbm.at[:, ks], s_out.at[c])

    def add_sides(k, carry):
        for e in range(5):
            middle = jnp.zeros((I - 4, J), f32)
            state[e, k] = state_in[e, k] + jnp.concatenate([RL[k, e], middle, RR[k, e]], axis=0)
        return carry

    rest = (pltpu.make_async_copy(shift, shift_hbm, s_out.at[HAND]),
            pltpu.make_async_copy(abl, abl_hbm, s_out.at[HAND + 1]))
    for copy in rest:
        copy.start()
    for c in range(HAND):
        lax.fori_loop(c * size, (c + 1) * size, add_sides, 0)
        store(c).start()
    for c in range(HAND):
        store(c).wait()
    for copy in rest:
        copy.wait()


def shards(flow_state, spacing, bc_kind, cell_of, zone_id, abl_temp, conduct, diffuse, rate):
    NT = lax.axis_size("surf")
    W = lax.axis_size("wall")
    K, I, J = spacing.shape
    C = cell_of.shape[0]
    PT = -(-(C // NT) // 128) * 128
    R = I * J // 128
    count = NT * PT
    dims = (K, I, J, NT, W, C, PT, conduct.shape[0])
    dma = pltpu.SemaphoreType.DMA
    chunks = len(bounds_of(K)) - 1
    scratch = [
        pltpu.VMEM(flow_state.shape, f32),
        pltpu.VMEM(spacing.shape, f32),
        pltpu.VMEM(bc_kind.shape, jnp.int32),
        pltpu.VMEM((1, C), jnp.int32),
        pltpu.VMEM((1, C), jnp.int32),
        pltpu.VMEM(abl_temp.shape, f32),
        pltpu.SMEM(conduct.shape, f32),
        pltpu.SMEM(conduct.shape, f32),
        pltpu.SMEM(conduct.shape, f32),
        dma((chunks,)), dma((8,)),
        pltpu.VMEM((K + 4, 5, I, J), f32),
        pltpu.VMEM((K + 4, 4, I, J), f32),
        pltpu.VMEM((K, 5, 2, J), f32),
        pltpu.VMEM((K, 5, 2, J), f32),
        pltpu.VMEM((count, C), bf16),
        pltpu.VMEM((16, max(C, count)), f32),
        pltpu.VMEM((NT, 8, PT), f32),
        pltpu.VMEM((NT, 8, PT), f32),
        pltpu.VMEM((NT, 8, PT), f32),
        pltpu.VMEM((NT, 8, PT), f32),
        pltpu.VMEM((I, J), f32),
        pltpu.VMEM((W, I, J), f32),
        pltpu.VMEM((2, I, J), f32),
        pltpu.VMEM((2, I, J), f32),
        pltpu.VMEM((2, R, 128), f32),
        pltpu.VMEM((W, 2, R, 128), f32),
        pltpu.VMEM((2, 5, 2, I, J), f32),
        pltpu.VMEM((2, 2, I, J), f32),
        pltpu.VMEM((K + 4, I, J), f32),
        pltpu.VMEM((2, R, 128), f32),
        dma((NT,)), dma((NT,)), dma((NT,)), dma((NT,)),
        dma((W,)), dma((W,)), dma((W,)), dma,
        dma((W,)), dma((W,)),
        dma((2,)), dma((2,)), dma((2,)), dma((2,)),
        dma((2, chunks)), dma((2, chunks)),
    ]
    hbm = pl.BlockSpec(memory_space=pltpu.HBM)
    vmem = pl.BlockSpec(memory_space=pltpu.VMEM)
    held = [pltpu.with_memory_space_constraint(x, pltpu.HBM) for x in (
        flow_state, spacing, bc_kind, cell_of.reshape(1, C), zone_id.reshape(1, C), abl_temp,
        conduct, diffuse, rate)]
    results = pl.pallas_call(
        functools.partial(kernel, dims),
        out_shape=(
            jax.ShapeDtypeStruct(flow_state.shape, f32),
            jax.ShapeDtypeStruct(spacing.shape, f32),
            jax.ShapeDtypeStruct(abl_temp.shape, f32),
            jax.ShapeDtypeStruct((K, 5, 2, J), f32),
            jax.ShapeDtypeStruct((K, 5, 2, J), f32),
        ),
        in_specs=[hbm] * 9,
        out_specs=(vmem,) * 5,
        scratch_shapes=scratch,
        compiler_params=pltpu.CompilerParams(
            collective_id=0, has_side_effects=True, vmem_limit_bytes=VMEM_BYTES),
    )(*held)
    return pl.pallas_call(
        hand_out,
        out_shape=[jax.ShapeDtypeStruct(r.shape, f32) for r in results[:3]],
        in_specs=[vmem] * 5,
        out_specs=[hbm] * 3,
        scratch_shapes=[pltpu.VMEM(flow_state.shape, f32), dma((HAND + 2,))],
        compiler_params=pltpu.CompilerParams(vmem_limit_bytes=VMEM_BYTES),
    )(*results)


def solution(mesh):
    in_specs = (
        P(None, "wall", "surf", None),
        P("wall", "surf", None),
        P("surf", None),
        P(("surf", "wall")),
        P(("surf", "wall")),
        P(None, ("surf", "wall")),
        P(),
        P(),
        P(),
    )
    out_specs = (P(None, "wall", "surf", None), P("wall", "surf", None), P(None, ("surf", "wall")))
    return jax.shard_map(shards, mesh=mesh, in_specs=in_specs, out_specs=out_specs, check_vma=False)
```

```python
import functools

import jax
import jax.numpy as jnp
from jax import lax
from jax.experimental import pallas as pl
from jax.experimental.pallas import tpu as pltpu
from jax.sharding import PartitionSpec as P

f32 = jnp.float32
bf16 = jnp.bfloat16
MESH = pl.DeviceIdType.MESH

time_step = 0.15
viscosity = 0.05
conduction = 0.07
sponge_rate = 0.5
far_values = (1.0, 0.5, 0.0, 0.0, 2.625)
SCALE = time_step / 12.0
CHUNK = 4
HAND = 4
VMEM_BYTES = 26 * 1024 * 1024


def bounds_of(K):
    return (0, 2) + tuple(range(4, K + 1, CHUNK))


def parts3(x):
    a = x.astype(bf16).astype(f32)
    b = (x - a).astype(bf16).astype(f32)
    c = (x - a - b).astype(bf16).astype(f32)
    return a, b, c


def shift_of(n):
    assert n & (n - 1) == 0
    return n.bit_length() - 1


def pick(index, table_ref, count):
    out = jnp.zeros(index.shape, f32)
    for z in range(count):
        out = jnp.where(index == z, table_ref[z], out)
    return out


def normal_fields(density, vx, vy, vz, pressure):
    energy = 2.5 * pressure + 0.5 * density * (vx * vx + vy * vy + vz * vz)
    svz = SCALE * vz
    rho_w = density * svz
    flux = (
        rho_w,
        rho_w * vx,
        rho_w * vy,
        rho_w * vz + SCALE * pressure,
        (energy + pressure) * svz,
    )
    cv = SCALE * viscosity
    return flux, (cv * vx, cv * vy, cv * vz, (SCALE * conduction) * (pressure / density))


def primitives_of(u0, u1, u2, u3, u4):
    inv = 1.0 / u0
    vx, vy, vz = u1 * inv, u2 * inv, u3 * inv
    pressure = 0.4 * (u4 - 0.5 * (u1 * vx + u2 * vy + u3 * vz))
    return inv, vx, vy, vz, pressure


def kernel(
    dims,
    flow_hbm, spacing_hbm, kind_hbm, cells_hbm, zones_hbm, abl_hbm, conduct_hbm, diffuse_hbm, rate_hbm,
    out, shift_out, abl_out, RL, RR,
    flow, spacing, kind, cells, zones, abl, conduct, diffuse, rate, s_flow, s_in,
    F3, Q, XR, XL, PM, V, send_list, recv_list, reply, reply_in,
    slab_total, totals_in, film_buf, film_in, part, part_in,
    halo_u, halo_s, sp, dense,
    s_list, r_list, s_rep, r_rep, s_tot, r_tot, s_film, r_film, s_part, r_part,
    s_hu, r_hu, s_hs, r_hs, s_x, r_x,
):
    K, I, J, NT, W, C, PT, NZ = dims
    R = I * J // 128
    JB = J // 128
    s = lax.axis_index("surf")
    w = lax.axis_index("wall")

    cuts = bounds_of(K)
    chunks = len(cuts) - 1

    def flow_copy(c):
        ks = pl.ds(cuts[c], cuts[c + 1] - cuts[c])
        return pltpu.make_async_copy(flow_hbm.at[:, ks], flow.at[:, ks], s_flow.at[c])

    pairs = ((spacing_hbm, spacing), (cells_hbm, cells), (zones_hbm, zones), (abl_hbm, abl),
             (kind_hbm, kind), (conduct_hbm, conduct), (diffuse_hbm, diffuse), (rate_hbm, rate))
    inputs = [pltpu.make_async_copy(a, b, s_in.at[n]) for n, (a, b) in enumerate(pairs)]
    flow_copy(0).start()
    barrier = pltpu.get_barrier_semaphore()
    for d in range(1, NT):
        pl.semaphore_signal(barrier, inc=1, device_id=(lax.rem(s + d, NT), w), device_id_type=MESH)
    for d in range(1, W):
        pl.semaphore_signal(barrier, inc=1, device_id=(s, lax.rem(w + d, W)), device_id_type=MESH)
    for copy in inputs:
        copy.start()
    for c in range(1, chunks):
        flow_copy(c).start()

    def list_copy(d):
        t = lax.rem(s + d, NT)
        return pltpu.make_async_remote_copy(
            send_list.at[t], recv_list.at[d], s_list.at[d], r_list.at[d],
            device_id=(t, w), device_id_type=MESH)

    def total_copy(d):
        return pltpu.make_async_remote_copy(
            slab_total, totals_in.at[w], s_tot.at[d], r_tot.at[d],
            device_id=(s, lax.rem(w + d, W)), device_id_type=MESH)

    def film_copy(d):
        return pltpu.make_async_remote_copy(
            film_buf, film_in, s_film.at[d], r_film,
            device_id=(s, lax.rem(w + d, W)), device_id_type=MESH)

    def halo_copies(side):
        near, target = (K - 2, lax.rem(w + 1, W)) if side == 0 else (0, lax.rem(w + W - 1, W))
        return (
            pltpu.make_async_remote_copy(
                flow_hbm.at[:, near : near + 2], halo_u.at[side], s_hu.at[side], r_hu.at[side],
                device_id=(s, target), device_id_type=MESH),
            pltpu.make_async_remote_copy(
                spacing_hbm.at[near : near + 2], halo_s.at[side], s_hs.at[side], r_hs.at[side],
                device_id=(s, target), device_id_type=MESH),
        )

    def side_copies(c):
        ks = pl.ds(cuts[c], cuts[c + 1] - cuts[c])
        return (
            pltpu.make_async_remote_copy(
                XR.at[ks], RL.at[ks], s_x.at[0, c], r_x.at[0, c],
                device_id=(lax.rem(s + 1, NT), w), device_id_type=MESH),
            pltpu.make_async_remote_copy(
                XL.at[ks], RR.at[ks], s_x.at[1, c], r_x.at[1, c],
                device_id=(lax.rem(s + NT - 1, NT), w), device_id_type=MESH),
        )

    i_row = lax.broadcasted_iota(jnp.int32, (I, J), 0)

    def surface_terms(k, carry):
        u = [flow[e, k] for e in range(5)]
        inv, vx, vy, vz, pressure = primitives_of(*u)
        enthalpy = u[4] + pressure
        sx, sy, sz, sp_ = SCALE * vx, SCALE * vy, SCALE * vz, SCALE * pressure
        m12, m13, m23 = u[1] * sy, u[1] * sz, u[2] * sz
        q = (viscosity * sx, viscosity * sy, viscosity * sz,
             (conduction * inv) * sp_)
        f1 = (SCALE * u[1], u[1] * sx + sp_, m12, m13, enthalpy * sx)
        f2 = (SCALE * u[2], m12, u[2] * sy + sp_, m23, enthalpy * sy)
        f3 = (SCALE * u[3], m13, m23, u[3] * sz + sp_, enthalpy * sz)
        for e in range(5):
            F3[k + 2, e] = f3[e]
        for e in range(4):
            Q[k + 2, e] = q[e]
        for e in range(5):
            total = u[e]
            if e:
                qe = q[e - 1]
                total = total - 60.0 * qe
                q8 = 8.0 * qe
            for axis, size, flux in ((0, I, f1[e]), (1, J, f2[e])):
                if e:
                    up2 = flux - qe
                    down2 = -flux - qe
                    up1 = q8 - 8.0 * up2
                    down1 = q8 - 8.0 * down2
                else:
                    up2 = flux
                    down2 = -flux
                    up1 = -8.0 * flux
                    down1 = 8.0 * flux
                r1 = pltpu.roll(down1, 1, axis)
                r2 = pltpu.roll(down2, 2, axis)
                l1 = pltpu.roll(up1, size - 1, axis)
                l2 = pltpu.roll(up2, size - 2, axis)
                if axis == 0:
                    to_right = r2 + jnp.where(i_row == 0, r1, 0.0)
                    to_left = up2 + jnp.where(i_row == 1, pltpu.roll(up1, 1, 0), 0.0)
                    XR[k, e] = to_right[0:2]
                    XL[k, e] = to_left[0:2]
                    r1 = jnp.where(i_row >= 1, r1, 0.0)
                    r2 = jnp.where(i_row >= 2, r2, 0.0)
                    l1 = jnp.where(i_row <= I - 2, l1, 0.0)
                    l2 = jnp.where(i_row <= I - 3, l2, 0.0)
                total = total + ((r1 + r2) + (l1 + l2))
            out[e, k] = total
        return carry

    def chunk(c, send=True):
        flow_copy(c).wait()
        lax.fori_loop(cuts[c], cuts[c + 1], surface_terms, 0)
        if send:
            for copy in side_copies(c):
                copy.start()

    chunk(0, send=False)
    pl.semaphore_wait(barrier, NT - 1 + W - 1)
    for copy in side_copies(0):
        copy.start()
    @pl.when(w < W - 1)
    def _():
        for copy in halo_copies(0):
            copy.start()

    @pl.when(w > 0)
    def _():
        for copy in halo_copies(1):
            copy.start()

    chunk(1)

    for copy in inputs[1:]:
        copy.wait()
    cell = cells[...]
    tile = lax.shift_right_logical(cell, shift_of(I * J))
    within = jnp.bitwise_and(cell, I * J - 1)
    row_i = lax.shift_right_logical(within, shift_of(J))
    col_j = jnp.bitwise_and(within, J - 1)
    row = lax.shift_right_logical(col_j, 7) * I + row_i
    lane = jnp.bitwise_and(col_j, 127)
    zone = zones[...]
    tile_iota = lax.broadcasted_iota(jnp.int32, (NT, C), 0)
    lane_iota = lax.broadcasted_iota(jnp.int32, (NT, C), 1)
    mine = jnp.where(tile_iota == tile, 1.0, 0.0).astype(f32)
    run = mine
    step = 1
    while step < C:
        run = run + jnp.where(lane_iota >= step, pltpu.roll(run, step, 1), 0.0)
        step *= 2
    rank = jnp.sum(mine * run, axis=0, keepdims=True).astype(jnp.int32) - 1
    slot = tile * PT + rank
    V[...] = jnp.zeros(V.shape, f32)
    V[0:1, 0:C] = row.astype(f32)
    V[1:2, 0:C] = lane.astype(f32)
    V[2:3, 0:C] = zone.astype(f32)
    for n, piece in enumerate(parts3(abl[0:1, :]) + parts3(abl[1:2, :])):
        V[3 + n : 4 + n, 0:C] = piece
    payload = V[:, 0:C].astype(bf16)
    slot_iota = lax.broadcasted_iota(jnp.int32, (PT, C), 0)
    for t in range(NT):
        block = jnp.where(slot_iota + t * PT == slot, 1.0, 0.0).astype(bf16)
        PM[t * PT : (t + 1) * PT, :] = block
        got = lax.dot_general(payload, block, (((1,), (1,)), ((), ())), preferred_element_type=f32)
        send_list[t] = jnp.zeros((8, PT), f32)
        send_list[t, 0:3] = got[0:3]
        send_list[t, 3:4] = got[3:4] + got[4:5] + got[5:6]
        send_list[t, 4:5] = got[6:7] + got[7:8] + got[8:9]

    for d in range(1, NT):
        list_copy(d).start()

    inputs[0].wait()
    def add_total(k, total):
        layer = spacing[k]
        sp[k + 2] = layer
        return total + layer

    slab_total[...] = lax.fori_loop(0, K, add_total, jnp.zeros((I, J), f32))
    inv, vx, vy, vz, pressure = primitives_of(*[flow[e, 0] for e in range(5)])
    film_buf[0] = 2.0 / spacing[0]
    film_buf[1] = pressure * inv + 0.2 * (vx * vx + vy * vy + vz * vz)

    @pl.when(w == 0)
    def _():
        for d in range(1, W):
            film_copy(d).start()

    for d in range(1, W):
        total_copy(d).start()
    totals_in[w] = slab_total[...]

    for c in (2, 3, 4, 5):
        chunk(c)

    recv_list[0] = send_list[s]
    for d in range(1, NT):
        list_copy(d).wait()
    listed = jnp.concatenate([recv_list[d] for d in range(NT)], axis=1)
    count = NT * PT
    l_row = listed[0:1].astype(jnp.int32)
    l_lane = listed[1:2].astype(jnp.int32)
    row_hot = jnp.where(lax.broadcasted_iota(jnp.int32, (R, count), 0) == l_row, 1.0, 0.0)
    lane_hot = jnp.where(
        lax.broadcasted_iota(jnp.int32, (128, count), 0) == l_lane, 1.0, 0.0).astype(bf16)
    pieces = parts3(listed[3:4]) + parts3(listed[4:5]) + (listed[2:3],)
    stack = jnp.concatenate([row_hot * piece for piece in pieces], axis=0).astype(bf16)
    grid = lax.dot_general(stack, lane_hot, (((1,), (1,)), ((), ())), preferred_element_type=f32)
    first = grid[0:R] + grid[R : 2 * R] + grid[2 * R : 3 * R]
    second = grid[3 * R : 4 * R] + grid[4 * R : 5 * R] + grid[5 * R : 6 * R]
    zone_grid = grid[6 * R : 7 * R]

    @pl.when(w == 0)
    def _():
        for d in range(1, W):
            film_copy(d).wait_send()
        film_in[...] = film_buf[...]

    @pl.when(w > 0)
    def _():
        film_copy(1).wait_recv()

    film = jnp.concatenate([film_in[0, :, b * 128 : (b + 1) * 128] for b in range(JB)], axis=0)
    recov = jnp.concatenate([film_in[1, :, b * 128 : (b + 1) * 128] for b in range(JB)], axis=0)
    zone_grid = zone_grid.astype(jnp.int32)
    owned = first > 0.25
    cond = pick(zone_grid, conduct, NZ)
    surface = jnp.where(owned, first, 1.0)
    for newton_pass in range(2):
        cube = surface * surface * surface
        surface = (film * recov + cond * second + 2.4 * cube * surface) / (film + cond + 3.2 * cube)
    recess = pick(zone_grid, rate, NZ) * jnp.exp(-2.0 / surface)
    part[0] = jnp.where(owned, surface, 0.0)
    part[1] = jnp.where(owned, recess, 0.0)

    def part_copy(d):
        return pltpu.make_async_remote_copy(
            part, part_in.at[d], s_part.at[d], r_part.at[d],
            device_id=(s, lax.rem(w + d, W)), device_id_type=MESH)

    for d in range(1, W):
        part_copy(d).start()

    table = jnp.concatenate(parts3(part[0]), axis=0).astype(bf16)
    spread = jnp.dot(table, lane_hot, preferred_element_type=f32)
    spread = spread[0:R] + spread[R : 2 * R] + spread[2 * R : 3 * R]
    answer = jnp.sum(spread * row_hot, axis=0, keepdims=True)
    for d in range(NT):
        reply[d] = jnp.broadcast_to(answer[:, d * PT : (d + 1) * PT], (8, PT))

    def reply_copy(d):
        return pltpu.make_async_remote_copy(
            reply.at[d], reply_in.at[s], s_rep.at[d], r_rep.at[d],
            device_id=(lax.rem(s + NT - d, NT), w), device_id_type=MESH)

    for d in range(1, NT):
        reply_copy(d).start()
    reply_in[s] = reply[0]
    for c in range(6, chunks):
        chunk(c)

    for d in range(1, NT):
        reply_copy(d).wait()
    answer = jnp.concatenate([reply_in[t, 0:1] for t in range(NT)], axis=1)
    V[...] = jnp.zeros(V.shape, f32)
    for n, piece in enumerate(parts3(answer)):
        V[n : n + 1, 0:count] = piece
    back = jnp.dot(V[:, 0:count].astype(bf16), PM[...], preferred_element_type=f32)
    col_surface = back[0:1] + back[1:2] + back[2:3]
    col_diffuse = pick(zone, diffuse, NZ)
    depth = abl.shape[0]
    depth_row = lax.broadcasted_iota(jnp.int32, (depth, C), 0)
    profile = jnp.where(depth_row == 0, col_surface, abl[...])
    for heat_pass in range(2):
        below = pltpu.roll(profile, 1, 0)
        above = jnp.where(depth_row == depth - 1, below, pltpu.roll(profile, depth - 1, 0))
        gain = col_diffuse * (above - 2.0 * profile + below)
        profile = jnp.where(depth_row == 0, profile, profile + gain)
    abl_out[...] = profile

    for d in range(1, W):
        part_copy(d).wait()
    whole = part[...]
    for d in range(1, W):
        whole = whole + part_in[d]
    dense[...] = whole
    surf_temp = jnp.concatenate([dense[0, b * I : (b + 1) * I, :] for b in range(JB)], axis=1)
    surf_recess = jnp.concatenate([dense[1, b * I : (b + 1) * I, :] for b in range(JB)], axis=1)

    for d in range(1, W):
        total_copy(d).wait()
    column_total = jnp.zeros((I, J), f32)
    offset = jnp.zeros((I, J), f32)
    for n in range(W):
        column_total = column_total + totals_in[n]
        offset = offset + jnp.where(n < w, totals_in[n], 0.0)

    @pl.when(w < W - 1)
    def _():
        for copy in halo_copies(0):
            copy.wait_send()
        for copy in halo_copies(1):
            copy.wait_recv()

    @pl.when(w > 0)
    def _():
        for copy in halo_copies(1):
            copy.wait_send()
        for copy in halo_copies(0):
            copy.wait_recv()

    def put(at, values):
        flux, fields = values
        for e in range(5):
            F3[at, e] = flux[e]
        for e in range(4):
            Q[at, e] = fields[e]

    def put_halo(side, base):
        for n in range(2):
            u = [halo_u[side, e, n] for e in range(5)]
            inv, vx, vy, vz, pressure = primitives_of(*u)
            put(base + n, normal_fields(u[0], vx, vy, vz, pressure))
            sp[base + n] = halo_s[side, n]

    @pl.when(w > 0)
    def _():
        put_halo(0, 0)

    @pl.when(w < W - 1)
    def _():
        put_halo(1, K + 2)

    @pl.when(w == 0)
    def _():
        kinds = kind[...]
        slip = kinds == 1
        for n in range(2):
            u = [flow[e, n] for e in range(5)]
            inv, vx, vy, vz, pressure = primitives_of(*u)
            density = jnp.where(slip, u[0], pressure / surf_temp)
            vx = jnp.where(slip, vx, -vx)
            vy = jnp.where(slip, vy, -vy)
            vz = jnp.where(kinds == 2, 2.0 * surf_recess - vz, -vz)
            put(1 - n, normal_fields(density, vx, vy, vz, pressure))
        sp[1] = spacing[1]
        sp[0] = spacing[0]

    @pl.when(w == W - 1)
    def _():
        one = jnp.full((I, J), 1.0, f32)
        zero = jnp.zeros((I, J), f32)
        for n in range(2):
            put(K + 2 + n, normal_fields(one, 0.5 * one, zero, zero, one))
        sp[K + 2] = spacing[K - 2]
        sp[K + 3] = spacing[K - 1]

    inv_total = 1.0 / column_total
    stretch = (1.0 + surf_recess * inv_total) * (1.0 / 12.0)

    def normal_terms(k, run):
        here = sp[k + 2]
        metric = stretch * (
            3.0 * (sp[k + 1] + sp[k + 3]) + 7.0 * here - 0.5 * (sp[k] + sp[k + 4]))
        inv_metric = 1.0 / metric
        inv_square = inv_metric * inv_metric
        normalized = (run + 0.5 * here) * inv_total
        shift_out[k] = surf_recess * (normalized - 1.0)
        damp = (time_step * sponge_rate) * normalized * normalized
        for e in range(5):
            diff = 8.0 * (F3[k + 3, e] - F3[k + 1, e]) - (F3[k + 4, e] - F3[k, e])
            total = out[e, k] - inv_metric * diff - damp * (flow[e, k] - far_values[e])
            if e:
                lap = (16.0 * (Q[k + 3, e - 1] + Q[k + 1, e - 1])
                       - (Q[k + 4, e - 1] + Q[k, e - 1]) - 30.0 * Q[k + 2, e - 1])
                total = total + inv_square * lap
            out[e, k] = total
        return run + here

    lax.fori_loop(0, K, normal_terms, offset)

    for c in range(chunks):
        for copy in side_copies(c):
            copy.wait()


def hand_out(state_in, shift, abl, RL, RR, state_hbm, shift_hbm, abl_hbm, state, s_out):
    K, I, J = state.shape[1:]
    size = K // HAND

    def store(c):
        ks = pl.ds(c * size, size)
        return pltpu.make_async_copy(state.at[:, ks], state_hbm.at[:, ks], s_out.at[c])

    def add_sides(k, carry):
        for e in range(5):
            middle = jnp.zeros((I - 4, J), f32)
            state[e, k] = state_in[e, k] + jnp.concatenate([RL[k, e], middle, RR[k, e]], axis=0)
        return carry

    rest = (pltpu.make_async_copy(shift, shift_hbm, s_out.at[HAND]),
            pltpu.make_async_copy(abl, abl_hbm, s_out.at[HAND + 1]))
    for copy in rest:
        copy.start()
    for c in range(HAND):
        lax.fori_loop(c * size, (c + 1) * size, add_sides, 0)
        store(c).start()
    for c in range(HAND):
        store(c).wait()
    for copy in rest:
        copy.wait()


def shards(flow_state, spacing, bc_kind, cell_of, zone_id, abl_temp, conduct, diffuse, rate):
    NT = lax.axis_size("surf")
    W = lax.axis_size("wall")
    K, I, J = spacing.shape
    C = cell_of.shape[0]
    PT = -(-(C // NT) // 128) * 128
    R = I * J // 128
    count = NT * PT
    dims = (K, I, J, NT, W, C, PT, conduct.shape[0])
    dma = pltpu.SemaphoreType.DMA
    chunks = len(bounds_of(K)) - 1
    scratch = [
        pltpu.VMEM(flow_state.shape, f32),
        pltpu.VMEM(spacing.shape, f32),
        pltpu.VMEM(bc_kind.shape, jnp.int32),
        pltpu.VMEM((1, C), jnp.int32),
        pltpu.VMEM((1, C), jnp.int32),
        pltpu.VMEM(abl_temp.shape, f32),
        pltpu.SMEM(conduct.shape, f32),
        pltpu.SMEM(conduct.shape, f32),
        pltpu.SMEM(conduct.shape, f32),
        dma((chunks,)), dma((8,)),
        pltpu.VMEM((K + 4, 5, I, J), f32),
        pltpu.VMEM((K + 4, 4, I, J), f32),
        pltpu.VMEM((K, 5, 2, J), f32),
        pltpu.VMEM((K, 5, 2, J), f32),
        pltpu.VMEM((count, C), bf16),
        pltpu.VMEM((16, max(C, count)), f32),
        pltpu.VMEM((NT, 8, PT), f32),
        pltpu.VMEM((NT, 8, PT), f32),
        pltpu.VMEM((NT, 8, PT), f32),
        pltpu.VMEM((NT, 8, PT), f32),
        pltpu.VMEM((I, J), f32),
        pltpu.VMEM((W, I, J), f32),
        pltpu.VMEM((2, I, J), f32),
        pltpu.VMEM((2, I, J), f32),
        pltpu.VMEM((2, R, 128), f32),
        pltpu.VMEM((W, 2, R, 128), f32),
        pltpu.VMEM((2, 5, 2, I, J), f32),
        pltpu.VMEM((2, 2, I, J), f32),
        pltpu.VMEM((K + 4, I, J), f32),
        pltpu.VMEM((2, R, 128), f32),
        dma((NT,)), dma((NT,)), dma((NT,)), dma((NT,)),
        dma((W,)), dma((W,)), dma((W,)), dma,
        dma((W,)), dma((W,)),
        dma((2,)), dma((2,)), dma((2,)), dma((2,)),
        dma((2, chunks)), dma((2, chunks)),
    ]
    hbm = pl.BlockSpec(memory_space=pltpu.HBM)
    vmem = pl.BlockSpec(memory_space=pltpu.VMEM)
    held = [pltpu.with_memory_space_constraint(x, pltpu.HBM) for x in (
        flow_state, spacing, bc_kind, cell_of.reshape(1, C), zone_id.reshape(1, C), abl_temp,
        conduct, diffuse, rate)]
    results = pl.pallas_call(
        functools.partial(kernel, dims),
        out_shape=(
            jax.ShapeDtypeStruct(flow_state.shape, f32),
            jax.ShapeDtypeStruct(spacing.shape, f32),
            jax.ShapeDtypeStruct(abl_temp.shape, f32),
            jax.ShapeDtypeStruct((K, 5, 2, J), f32),
            jax.ShapeDtypeStruct((K, 5, 2, J), f32),
        ),
        in_specs=[hbm] * 9,
        out_specs=(vmem,) * 5,
        scratch_shapes=scratch,
        compiler_params=pltpu.CompilerParams(
            collective_id=0, has_side_effects=True, vmem_limit_bytes=VMEM_BYTES),
    )(*held)
    return pl.pallas_call(
        hand_out,
        out_shape=[jax.ShapeDtypeStruct(r.shape, f32) for r in results[:3]],
        in_specs=[vmem] * 5,
        out_specs=[hbm] * 3,
        scratch_shapes=[pltpu.VMEM(flow_state.shape, f32), dma((HAND + 2,))],
        compiler_params=pltpu.CompilerParams(vmem_limit_bytes=VMEM_BYTES),
    )(*results)


def solution(mesh):
    in_specs = (
        P(None, "wall", "surf", None),
        P("wall", "surf", None),
        P("surf", None),
        P(("surf", "wall")),
        P(("surf", "wall")),
        P(None, ("surf", "wall")),
        P(),
        P(),
        P(),
    )
    out_specs = (P(None, "wall", "surf", None), P("wall", "surf", None), P(None, ("surf", "wall")))
    return jax.shard_map(shards, mesh=mesh, in_specs=in_specs, out_specs=out_specs, check_vma=False)
```
